32 devices in a mesh: dp: 4 (over z), row: 2 (over x), col: 4 (over y, core).
Axes of the slice: x: 2, y: 2, z: 4, core: 2. Of those that a mesh axis runs over, the one named last changes fastest.
Arguments:
- inputs: bfloat16 [16384, 768], P(('dp', 'row', 'col')), may hold values from -6 to 6
- pre_attn_gain: bfloat16 [768], replicated, may hold values from 0.25 to 1.75
- pre_attn_shift: bfloat16 [768], replicated, may hold values from -1.75 to 1.75
- qkv_weight: bfloat16 [768, 3, 768], P('row', None, 'col'), may hold values from -0.3125 to 0.3125
- qv_bias: bfloat16 [2, 768], P(None, 'col'), may hold values from -3 to 3
- out_weight: bfloat16 [768, 768], P('col', 'row'), may hold values from -1.75 to 1.75
- out_bias: bfloat16 [768], replicated, may hold values from -1.75 to 1.75
- pre_mlp_gain: bfloat16 [768], replicated, may hold values from 0.25 to 1.75
- pre_mlp_shift: bfloat16 [768], replicated, may hold values from -1.75 to 1.75
- fc_weight: bfloat16 [768, 3072], P('row', 'col'), may hold values from -0.21875 to 0.21875
- fc_bias: bfloat16 [3072], P('col'), may hold values from -3 to 3
- proj_weight: bfloat16 [3072, 768], P('col', 'row'), may hold values from -0.109375 to 0.109375
- proj_bias: bfloat16 [768], replicated, may hold values from -1.75 to 1.75
- cotangent: bfloat16 [16384, 768], P(('dp', 'row', 'col')), may hold values from -6 to 6
Outputs:
- block_out: bfloat16 [16384, 768], P(('dp', 'row', 'col'))
- input_grad: bfloat16 [16384, 768], P(('dp', 'row', 'col'))
- grad_pre_attn_gain: float32 [768], replicated
- grad_pre_attn_shift: float32 [768], replicated
- grad_qkv_weight: float32 [768, 3, 768], P('row', None, 'col')
- grad_qv_bias: float32 [2, 768], P(None, 'col')
- grad_out_weight: float32 [768, 768], P('col', 'row')
- grad_out_bias: float32 [768], replicated
- grad_pre_mlp_gain: float32 [768], replicated
- grad_pre_mlp_shift: float32 [768], replicated
- grad_fc_weight: float32 [768, 3072], P('row', 'col')
- grad_fc_bias: float32 [3072], P('col')
- grad_proj_weight: float32 [3072, 768], P('col', 'row')
- grad_proj_bias: float32 [768], replicated
The draws below stay inside these ranges and needn't reach their ends.
All inputs are finite; a program needn't handle non-finite values.
Results may differ from the reference program's by a relative error of at most 0.013.
The reference program's roundings to bfloat16 on the way count: a program that leaves them out, or rounds other values in their place, can miss the bound.
Values may be sent and summed in bfloat16 or wider, within the bound.
No kernel may reach another device: no remote copies, remote signals or barrier semaphores. Data moves between devices by JAX's collectives and lax.ppermute only.
A program may use at most 128 MiB of HBM per device.

```python
import jax
import jax.numpy as jnp
from jax import lax

D = 768
HEADS = 12
HEAD_DIM = 64
FF = 3072
SEQ_LEN = 2048
TOKENS = 16384


def shard_levels(stream_key, dims, pieces, low, largest):
    factor_of = 1.0
    for dim, shards_of in pieces:
        heights = jax.random.uniform(jax.random.fold_in(jax.random.fold_in(stream_key, 6), dim), (shards_of,), jnp.float32, low / len(pieces), largest / len(pieces))
        factor_of = factor_of * jnp.repeat(jnp.exp(heights), dims[dim] // shards_of).reshape((-1,) + (1,) * (len(dims) - 1 - dim))
    return factor_of


def bell_draw(key, shape, spread, most, cuts=(), kind=jnp.bfloat16):
    entries = jax.random.normal(key, shape, jnp.float32) * spread
    if len(cuts) > 0:
        entries = shard_levels(key, shape, cuts, -0.22, 0.18) * entries
    return jnp.clip(entries, min=-most, max=most).astype(kind)


def setup_inputs(seed: int = 0) -> dict:
    key_list = jax.random.split(jax.random.key(seed), 15)
    return {
        "inputs": bell_draw(key_list[0], (TOKENS, D), 1.0, 6.0, ((0, 32),)),
        "pre_attn_gain": jnp.clip(1.0 + 0.15 * jax.random.normal(key_list[1], (D,), jnp.float32), 0.25, 1.75).astype(jnp.bfloat16),
        "pre_attn_shift": bell_draw(key_list[2], (D,), 0.3, 1.75),
        "qkv_weight": bell_draw(key_list[3], (D, 3, D), (D // 2) ** -0.5, 0.3125, ((0, 2), (2, 4))),
        "qv_bias": bell_draw(key_list[4], (2, D), 0.5, 3.0, ((1, 4),)),
        "out_weight": bell_draw(key_list[5], (D, D), (D // 64) ** -0.5, 1.75, ((0, 4), (1, 2))),
        "out_bias": bell_draw(key_list[6], (D,), 0.3, 1.75),
        "pre_mlp_gain": jnp.clip(1.0 + 0.15 * jax.random.normal(key_list[7], (D,), jnp.float32), 0.25, 1.75).astype(jnp.bfloat16),
        "pre_mlp_shift": bell_draw(key_list[8], (D,), 0.3, 1.75),
        "fc_weight": bell_draw(key_list[9], (D, FF), D ** -0.5, 0.21875, ((0, 2), (1, 4))),
        "fc_bias": bell_draw(key_list[10], (FF,), 0.5, 3.0, ((0, 4),)),
        "proj_weight": bell_draw(key_list[11], (FF, D), FF ** -0.5, 0.109375, ((0, 4), (1, 2))),
        "proj_bias": bell_draw(key_list[12], (D,), 0.3, 1.75),
        "cotangent": bell_draw(key_list[13], (TOKENS, D), 1.0, 6.0, ((0, 32),)),
    }


@jax.custom_vjp
def low(v):
    return lax.optimization_barrier(v.astype(jnp.bfloat16)).astype(jnp.float32)

@jax.custom_vjp
def low_back(v):
    return v

def low_keep(v):
    return (low(v), None)

def low_pass(kept, grad):
    return (grad,)

def back_keep(v):
    return (v, None)

def back_low(kept, grad):
    return (low(grad),)
low.defvjp(low_keep, low_pass)
low_back.defvjp(back_keep, back_low)
eps = 1e-05
masked_score = -1e+30
highest = lax.Precision.HIGHEST

def layer_norm(rows, gain, shift):
    average = lax.optimization_barrier(jnp.mean(rows, axis=-1, keepdims=True))
    centred = rows - average
    variance = lax.optimization_barrier(jnp.mean(centred * centred, axis=-1, keepdims=True))
    return centred * lax.rsqrt(variance + eps) * gain + shift

def attend(queries, keys_seq, values_seq):
    seq_len = queries.shape[0]
    block_rows = min(512, seq_len)
    blocks = seq_len // block_rows
    score_scale = HEAD_DIM ** (-0.5)

    def one_block(block_index):
        first_row = block_index * block_rows
        query_block = lax.dynamic_slice_in_dim(queries, first_row, block_rows, 0)
        scores = low_back(jnp.einsum('qhd,khd->hqk', query_block, keys_seq, precision=highest) * score_scale)
        query_pos = first_row + jnp.arange(block_rows, dtype=jnp.int32)
        key_pos = jnp.arange(seq_len, dtype=jnp.int32)
        allowed = key_pos[None, :] <= query_pos[:, None]
        scores = jnp.where(allowed[None], scores, masked_score)
        row_max = lax.optimization_barrier(jnp.max(scores, axis=-1, keepdims=True))
        shifted = jnp.exp(scores - row_max)
        attn_probs = shifted / lax.optimization_barrier(jnp.sum(shifted, axis=-1, keepdims=True))
        return jnp.einsum('hqk,khd->qhd', low(attn_probs), values_seq, precision=highest)
    contexts = lax.map(jax.checkpoint(one_block), jnp.arange(blocks, dtype=jnp.int32))
    return contexts.reshape(seq_len, -1)

def forward(stream, pre_attn_gain, pre_attn_shift, qkv_weight, qv_bias, out_weight, out_bias, pre_mlp_gain, pre_mlp_shift, fc_weight, fc_bias, proj_weight, proj_bias):
    seq_len = stream.shape[0]
    normed_one = low(layer_norm(stream, pre_attn_gain, pre_attn_shift))
    bias_rows = jnp.stack([qv_bias[0], jnp.zeros_like(qv_bias[0]), qv_bias[1]])
    qkv_all = jnp.einsum('td,dje->tje', normed_one, qkv_weight, precision=highest) + bias_rows
    qkv_all = low(low_back(qkv_all))
    head_shape = (seq_len, HEADS, HEAD_DIM)
    context = attend(qkv_all[:, 0].reshape(head_shape), qkv_all[:, 1].reshape(head_shape), qkv_all[:, 2].reshape(head_shape))
    context = low(low_back(context))
    attn_out = low_back(jnp.dot(context, out_weight, precision=highest) + out_bias)
    mid_stream = stream + attn_out
    normed_two = low(layer_norm(mid_stream, pre_mlp_gain, pre_mlp_shift))
    pre_act = low_back(jnp.dot(normed_two, fc_weight, precision=highest) + fc_bias)
    hidden = low(jax.nn.gelu(pre_act, approximate=True))
    mlp_out = low_back(jnp.dot(hidden, proj_weight, precision=highest) + proj_bias)
    return mid_stream + mlp_out

def reference(inputs, pre_attn_gain, pre_attn_shift, qkv_weight, qv_bias, out_weight, out_bias, pre_mlp_gain, pre_mlp_shift, fc_weight, fc_bias, proj_weight, proj_bias, cotangent):
    params = tuple((parameter.astype(jnp.float32) for parameter in (pre_attn_gain, pre_attn_shift, qkv_weight, qv_bias, out_weight, out_bias, pre_mlp_gain, pre_mlp_shift, fc_weight, fc_bias, proj_weight, proj_bias)))
    seq_total = TOKENS // SEQ_LEN
    streams = inputs.astype(jnp.float32).reshape(seq_total, SEQ_LEN, D)
    out_grads = cotangent.astype(jnp.float32).reshape(seq_total, SEQ_LEN, D)

    def one_sequence(totals, seq_pair):
        stream, out_grad = seq_pair
        result, pullback = jax.vjp(forward, stream, *params)
        pulled = pullback(out_grad)
        totals = tuple((running + seq_part for running, seq_part in zip(totals, pulled[1:])))
        return (totals, (result, pulled[0]))
    start_totals = tuple((jnp.zeros_like(parameter) for parameter in params))
    totals, (results, stream_grads) = lax.scan(one_sequence, start_totals, (streams, out_grads))
    block_out = results.reshape(TOKENS, D).astype(jnp.bfloat16)
    input_grad = stream_grads.reshape(TOKENS, D).astype(jnp.bfloat16)
    return (block_out, input_grad, totals[0], totals[1], totals[2], totals[3], totals[4], totals[5], totals[6], totals[7], totals[8], totals[9], totals[10], totals[11])
```

```python
import functools
import jax
import jax.numpy as jnp
from jax import lax
from jax.experimental import pallas as pl
from jax.experimental.pallas import tpu as pltpu
from jax.sharding import PartitionSpec as P

HEAD_DIM = 64
masked_score = -1e30


def tile_start(tile, tile_rows, block_rows, here):
    per_block = block_rows // tile_rows
    return pl.multiple_of(
        (here ^ (tile // per_block)) * block_rows + tile % per_block * tile_rows, tile_rows
    )


def forward_kernel(here_ref, q_ref, k_ref, v_ref, low_ref, wide_ref, lse_ref, keys, *, block, tq, tk):
    here = here_ref[0]
    seq = q_ref.shape[1]
    keys[...] = k_ref[...].T
    for qi in range(seq // tq):
        q_at = tile_start(qi, tq, block, here)
        query = q_ref[:, pl.ds(q_at, tq)] * 0.125
        peak = total = acc = None
        for ki in range((qi + 1) * tq // tk if tq >= tk else qi * tq // tk + 1):
            k_at = tile_start(ki, tk, block, here)
            scores = jnp.dot(keys[pl.ds(k_at, tk), :], query, preferred_element_type=jnp.float32)
            if (ki + 1) * tk > qi * tq + 1:
                k_pos = ki * tk + lax.broadcasted_iota(jnp.int32, (tk, tq), 0)
                q_pos = qi * tq + lax.broadcasted_iota(jnp.int32, (tk, tq), 1)
                scores = jnp.where(k_pos <= q_pos, scores, masked_score)
            tile_peak = jnp.max(scores, axis=0, keepdims=True)
            new_peak = tile_peak if peak is None else jnp.maximum(peak, tile_peak)
            shifted = jnp.exp(scores - new_peak)
            tile_total = jnp.sum(shifted, axis=0, keepdims=True)
            part = jnp.dot(
                v_ref[:, pl.ds(k_at, tk)], shifted.astype(jnp.bfloat16),
                preferred_element_type=jnp.float32,
            )
            if peak is None:
                total, acc = tile_total, part
            else:
                shrink = jnp.exp(peak - new_peak)
                total = total * shrink + tile_total
                acc = acc * shrink + part
            peak = new_peak
        wide = acc / total
        wide_ref[:, pl.ds(q_at, tq)] = wide
        low_ref[:, pl.ds(q_at, tq)] = wide.astype(jnp.bfloat16)
        lse_ref[0, :, pl.ds(q_at, tq)] = peak + jnp.log(total)


def backward_kernel(
    here_ref, q_ref, k_ref, v_ref, g_ref, wide_ref, lse_ref, dq_ref, dk_ref, dv_ref,
    keys, values, queries, grads, dkeys, dvalues, *, block, tq, tk,
):
    here = here_ref[0]
    seq = q_ref.shape[1]
    keys[...] = k_ref[...].T
    values[...] = v_ref[...].T
    queries[...] = (q_ref[...] * 0.125).T
    grads[...] = g_ref[...].T
    for qi in range(seq // tq):
        q_at = tile_start(qi, tq, block, here)
        query = q_ref[:, pl.ds(q_at, tq)] * 0.125
        grad = g_ref[:, pl.ds(q_at, tq)]
        query_rows = queries[pl.ds(q_at, tq), :]
        grad_rows = grads[pl.ds(q_at, tq), :]
        lse = lse_ref[0, :, pl.ds(q_at, tq)]
        inner = jnp.sum(
            grad.astype(jnp.float32) * wide_ref[:, pl.ds(q_at, tq)], axis=0, keepdims=True
        )
        acc = None
        for ki in range((qi + 1) * tq // tk if tq >= tk else qi * tq // tk + 1):
            k_at = tile_start(ki, tk, block, here)
            k_rows = pl.ds(k_at, tk)
            scores = jnp.dot(keys[k_rows, :], query, preferred_element_type=jnp.float32)
            probs = jnp.exp(scores - lse)
            if (ki + 1) * tk > qi * tq + 1:
                k_pos = ki * tk + lax.broadcasted_iota(jnp.int32, (tk, tq), 0)
                q_pos = qi * tq + lax.broadcasted_iota(jnp.int32, (tk, tq), 1)
                probs = jnp.where(k_pos <= q_pos, probs, 0.0)
            prob_grad = jnp.dot(values[k_rows, :], grad, preferred_element_type=jnp.float32)
            score_grad = (probs * (prob_grad - inner)).astype(jnp.bfloat16)
            dv = jnp.dot(probs.astype(jnp.bfloat16), grad_rows, preferred_element_type=jnp.float32)
            dk = jnp.dot(score_grad, query_rows, preferred_element_type=jnp.float32)
            dq = jnp.dot(
                k_ref[:, k_rows], score_grad, preferred_element_type=jnp.float32
            )
            acc = dq if acc is None else acc + dq
            if qi * tq // tk * tk <= ki * tk and qi * tq % tk == 0:
                dkeys[k_rows, :] = dk
                dvalues[k_rows, :] = dv
            else:
                dkeys[k_rows, :] += dk
                dvalues[k_rows, :] += dv
        dq_ref[:, pl.ds(q_at, tq)] = (acc * 0.125).astype(jnp.bfloat16)
    dk_ref[...] = dkeys[...].T.astype(jnp.bfloat16)
    dv_ref[...] = dvalues[...].T.astype(jnp.bfloat16)


def attend_forward(here, qkv, block, tq=512, tk=512):
    feats, seq = qkv.shape
    heads = feats // 3 // HEAD_DIM
    part = lambda j: pl.BlockSpec((HEAD_DIM, seq), lambda h, _: (j * heads + h, 0))
    return pl.pallas_call(
        functools.partial(forward_kernel, block=block, tq=tq, tk=tk),
        out_shape=(
            jax.ShapeDtypeStruct((feats // 3, seq), jnp.bfloat16),
            jax.ShapeDtypeStruct((feats // 3, seq), jnp.float32),
            jax.ShapeDtypeStruct((heads, 1, seq), jnp.float32),
        ),
        grid_spec=pltpu.PrefetchScalarGridSpec(
            num_scalar_prefetch=1,
            grid=(heads,),
            in_specs=[part(0), part(1), part(2)],
            out_specs=(part(0), part(0), pl.BlockSpec((1, 1, seq), lambda h, _: (h, 0, 0))),
            scratch_shapes=[pltpu.VMEM((seq, HEAD_DIM), jnp.bfloat16)],
        ),
        compiler_params=pltpu.CompilerParams(vmem_limit_bytes=48 * 2**20),
        cost_estimate=pl.CostEstimate(
            flops=heads * seq * seq * 512, bytes_accessed=feats * seq * 5,
            transcendentals=heads * seq * seq // 2,
        ),
        name="attn_forward",
    )(here, qkv, qkv, qkv)


def attend_backward(here, qkv, grad, wide, lse, block, tq=512, tk=512, first=0, count=None):
    feats, seq = qkv.shape
    heads = feats // 3 // HEAD_DIM
    count = heads if count is None else count
    part = lambda j: pl.BlockSpec((HEAD_DIM, seq), lambda h, _: (j * heads + first + h, 0))
    done = pl.BlockSpec((HEAD_DIM, seq), lambda h, _: (h, 0))
    return pl.pallas_call(
        functools.partial(backward_kernel, block=block, tq=tq, tk=tk),
        out_shape=(jax.ShapeDtypeStruct((count * HEAD_DIM, seq), jnp.bfloat16),) * 3,
        grid_spec=pltpu.PrefetchScalarGridSpec(
            num_scalar_prefetch=1,
            grid=(count,),
            in_specs=[
                part(0), part(1), part(2), part(0), part(0),
                pl.BlockSpec((1, 1, seq), lambda h, _: (first + h, 0, 0)),
            ],
            out_specs=(done, done, done),
            scratch_shapes=[pltpu.VMEM((seq, HEAD_DIM), jnp.bfloat16)] * 4
            + [pltpu.VMEM((seq, HEAD_DIM), jnp.float32)] * 2,
        ),
        compiler_params=pltpu.CompilerParams(vmem_limit_bytes=48 * 2**20),
        cost_estimate=pl.CostEstimate(
            flops=count * seq * seq * 1280, bytes_accessed=count * seq * 64 * 18,
            transcendentals=count * seq * seq // 2,
        ),
        name="attn_backward",
    )(here, qkv, qkv, qkv, grad, wide, lse)


eps = 1e-05


def layer_norm(rows, gain, shift):
    average = jnp.mean(rows, axis=-1, keepdims=True)
    centred = rows - average
    variance = jnp.mean(centred * centred, axis=-1, keepdims=True)
    return centred * lax.rsqrt(variance + eps) * gain + shift


def gelu_tanh(values):
    return jax.nn.gelu(values, approximate=True)


def swap(value, axis, step):
    count = lax.axis_size(axis)
    return lax.ppermute(value, axis, [(i, i ^ step) for i in range(count)])


def gather_xor(value, axis):
    count = lax.axis_size(axis)
    held = {0: value}
    step = count // 2
    while step:
        held.update({r ^ step: swap(held[r], axis, step) for r in list(held)})
        step //= 2
    return [held[r] for r in range(count)]


def gather_row(value):
    index = lax.axis_index("row")
    parts = gather_xor(value, "row")
    if len(parts) == 2:
        return jnp.where(index == 0, jnp.stack(parts), jnp.stack(parts[::-1]))
    stacked = jnp.zeros((len(parts),) + value.shape, value.dtype)
    for step, part in enumerate(parts):
        stacked = lax.dynamic_update_index_in_dim(stacked, part, index ^ step, 0)
    return stacked


def scatter_row(stacked):
    index = lax.axis_index("row")
    total = lax.dynamic_index_in_dim(stacked, index, 0, keepdims=False).astype(jnp.float32)
    for step in range(1, stacked.shape[0]):
        part = lax.dynamic_index_in_dim(stacked, index ^ step, 0, keepdims=False)
        total = total + swap(part.astype(jnp.bfloat16), "row", step).astype(jnp.float32)
    return total


def sum_dp(block):
    count = lax.axis_size("dp")
    index = lax.axis_index("dp")
    pieces = block.reshape((count, block.shape[0] // count) + block.shape[1:])
    total = lax.dynamic_index_in_dim(pieces, index, 0, keepdims=False).astype(jnp.float32)
    for step in range(1, count):
        part = lax.dynamic_index_in_dim(pieces, index ^ step, 0, keepdims=False)
        total = total + swap(part.astype(jnp.bfloat16), "dp", step).astype(jnp.float32)
    total = total.astype(jnp.bfloat16)
    out = jnp.zeros(pieces.shape, jnp.float32)
    for step in range(count):
        part = total if step == 0 else swap(total, "dp", step)
        out = lax.dynamic_update_index_in_dim(out, part.astype(jnp.float32), index ^ step, 0)
    return out.reshape(block.shape)


def sum_small(value, axes):
    for axis in axes:
        step = 1
        while step < lax.axis_size(axis):
            value = value + swap(value, axis, step)
            step *= 2
    return value


def contract(left, right, left_dim, right_dim):
    return lax.dot_general(
        left, right, (((left_dim,), (right_dim,)), ((), ())), preferred_element_type=jnp.float32
    )


def scatter_col(near, far, rows):
    blocks = [near[:rows], near[rows:], far[:rows], far[rows:]]
    away = blocks[2].astype(jnp.float32) + swap(blocks[3], "col", 1).astype(jnp.float32)
    away = swap(away.astype(jnp.bfloat16), "col", 2).astype(jnp.float32)
    return blocks[0].astype(jnp.float32) + swap(blocks[1], "col", 1).astype(jnp.float32) + away


def body(
    inputs,
    pre_attn_gain,
    pre_attn_shift,
    qkv_weight,
    qv_bias,
    out_weight,
    out_bias,
    pre_mlp_gain,
    pre_mlp_shift,
    fc_weight,
    fc_bias,
    proj_weight,
    proj_bias,
    cotangent,
):
    low = jnp.bfloat16
    wide = jnp.float32
    rows, width = inputs.shape
    cols = lax.axis_size("col")
    row_count = lax.axis_size("row")
    row_index = lax.axis_index("row")
    here = lax.axis_index("col").astype(jnp.int32).reshape(1)
    head_cols = qkv_weight.shape[2]
    hidden_cols = fc_weight.shape[1]
    every = ("col", "row", "dp")
    gain_one, shift_one = pre_attn_gain.astype(wide), pre_attn_shift.astype(wide)
    gain_two, shift_two = pre_mlp_gain.astype(wide), pre_mlp_shift.astype(wide)

    stream = inputs.astype(wide)
    normed_one = layer_norm(stream, gain_one, shift_one).astype(low)
    normed = gather_xor(normed_one, "col")
    normed_near = jnp.concatenate(normed[:2], 0)
    normed_far = jnp.concatenate(normed[2:], 0)
    qkv_full = gather_row(qkv_weight.reshape(-1, 3 * head_cols)).reshape(width, 3 * head_cols)
    bias_wide = qv_bias.astype(wide)
    bias_col = jnp.concatenate([bias_wide[0], jnp.zeros_like(bias_wide[0]), bias_wide[1]])[:, None]
    qkv = jnp.concatenate(
        [
            (contract(qkv_full, part, 0, 1) + bias_col).astype(low)
            for part in (normed_near, normed_far)
        ],
        1,
    )
    context, context_wide, lse = attend_forward(here, qkv, rows)
    out_rows = jnp.moveaxis(gather_row(out_weight), 0, 1).reshape(head_cols, width)
    out_full = jnp.concatenate(gather_xor(out_rows, "col"), 0)
    context_own = jnp.concatenate(
        [
            context[:, :rows] if r == 0 else swap(context[:, r * rows : (r + 1) * rows], "col", r)
            for r in range(cols)
        ],
        0,
    )
    mid_stream = stream + contract(context_own, out_full, 0, 0) + out_bias.astype(wide)
    normed_two = layer_norm(mid_stream, gain_two, shift_two).astype(low)

    fc_full = gather_row(fc_weight).reshape(width, hidden_cols)
    proj_full = jnp.moveaxis(gather_row(proj_weight), 0, 1).reshape(hidden_cols, width)
    fc_bias_wide = fc_bias.astype(wide)
    cot = gather_xor(cotangent, "col")
    two = gather_xor(normed_two, "col")
    sides = []
    for first in (0, 2):
        normed_side = jnp.concatenate(two[first : first + 2], 0)
        cot_side = jnp.concatenate(cot[first : first + 2], 0)
        pre_act = contract(normed_side, fc_full, 1, 0) + fc_bias_wide
        hidden_wide, gelu_pull = jax.vjp(gelu_tanh, pre_act)
        hidden = hidden_wide.astype(low)
        pre_grad = gelu_pull(contract(cot_side, proj_full, 1, 1))[0].astype(low)
        two_grad = contract(pre_grad, fc_full, 1, 1).astype(low)
        mlp_out = contract(hidden, proj_full, 1, 0).astype(low)
        fc_grad = contract(normed_side, pre_grad, 0, 0)
        proj_grad = contract(cot_side, hidden, 0, 0)
        sides.append(
            (two_grad, mlp_out, fc_grad, proj_grad, jnp.sum(pre_grad, axis=0, dtype=wide))
        )
    near, far = sides
    normed_two_grad = scatter_col(near[0], far[0], rows)
    out_grad = cotangent.astype(wide)
    norm_two_pull = jax.vjp(layer_norm, mid_stream, gain_two, shift_two)[1]
    stream_two, gain_two_grad, shift_two_grad = norm_two_pull(normed_two_grad)
    mid_grad = out_grad + stream_two
    mid_low = mid_grad.astype(low)
    context_grad_own = contract(out_full, mid_low, 1, 1).astype(low)
    context_grad = jnp.concatenate(
        [
            context_grad_own[:head_cols]
            if r == 0
            else swap(context_grad_own[r * head_cols : (r + 1) * head_cols], "col", r)
            for r in range(cols)
        ],
        1,
    )
    mlp_sum = scatter_col(near[1], far[1], rows)
    block_out = (mid_stream + mlp_sum + proj_bias.astype(wide)).astype(low)
    fc_sum = sum_dp(scatter_row((near[2] + far[2]).reshape(row_count, -1, hidden_cols)))
    proj_sum = sum_dp(scatter_row((near[3] + far[3]).reshape(row_count, -1, hidden_cols))).T
    out_part = contract(context_own, mid_low, 1, 0)
    out_block = out_part[:head_cols]
    for r in range(1, cols):
        part = out_part[r * head_cols : (r + 1) * head_cols].astype(low)
        out_block = out_block + swap(part, "col", r).astype(wide)
    out_block = jnp.moveaxis(out_block.reshape(head_cols, row_count, -1), 1, 0)
    out_sum = sum_dp(scatter_row(out_block))
    early = jnp.stack(
        [
            jnp.sum(mid_low, axis=0, dtype=wide),
            gain_two_grad,
            shift_two_grad,
            jnp.sum(out_grad, axis=0),
        ]
    )
    early_sum = sum_small(early, every)
    fc_bias_sum = sum_small((near[4] + far[4]).reshape(1, -1), ("row", "dp"))[0]

    grads = attend_backward(here, qkv, context_grad, context_wide, lse, rows)
    qkv_grad = jnp.concatenate(grads, 0)
    qv_part = jnp.stack(
        [jnp.sum(grads[0], axis=1, dtype=wide), jnp.sum(grads[2], axis=1, dtype=wide)]
    )
    qv_sum = sum_small(qv_part, ("row", "dp"))
    weights = gather_xor(qkv_full, "col")
    normed_one_grad = 0.0
    for r in range(cols):
        part = qkv_grad[:, r * rows : (r + 1) * rows]
        part = part if r == 0 else swap(part, "col", r)
        normed_one_grad = normed_one_grad + contract(part, weights[r], 0, 1)
    qkv_part = contract(normed_near, qkv_grad[:, : 2 * rows], 0, 1)
    qkv_part = qkv_part + contract(normed_far, qkv_grad[:, 2 * rows :], 0, 1)
    qkv_sum = sum_dp(scatter_row(qkv_part.reshape(row_count, -1, 3 * head_cols)))
    norm_one_pull = jax.vjp(layer_norm, stream, gain_one, shift_one)[1]
    stream_one, gain_one_grad, shift_one_grad = norm_one_pull(normed_one_grad)
    input_grad = (mid_grad + stream_one).astype(low)
    late_sum = sum_small(jnp.stack([gain_one_grad, shift_one_grad]), every)
    return (
        block_out,
        input_grad,
        late_sum[0],
        late_sum[1],
        qkv_sum.reshape(qkv_weight.shape),
        qv_sum,
        out_sum,
        early_sum[0],
        early_sum[1],
        early_sum[2],
        fc_sum,
        fc_bias_sum,
        proj_sum,
        early_sum[3],
    )


def solution(mesh):
    placed = (
        P(("dp", "row", "col"), None),
        P(),
        P(),
        P("row", None, "col"),
        P(None, "col"),
        P("col", "row"),
        P(),
        P(),
        P(),
        P("row", "col"),
        P("col"),
        P("col", "row"),
        P(),
        P(("dp", "row", "col"), None),
    )
    return jax.shard_map(
        body,
        mesh=mesh,
        in_specs=placed,
        out_specs=(
            P(("dp", "row", "col"), None),
            P(("dp", "row", "col"), None),
            P(),
            P(),
            P("row", None, "col"),
            P(None, "col"),
            P("col", "row"),
            P(),
            P(),
            P(),
            P("row", "col"),
            P("col"),
            P("col", "row"),
            P(),
        ),
        check_vma=False,
    )
```

```python
import functools
import jax
import jax.numpy as jnp
from jax import lax
from jax.experimental import pallas as pl
from jax.experimental.pallas import tpu as pltpu
from jax.sharding import PartitionSpec as P

HEAD_DIM = 64
masked_score = -1e30


def tile_start(tile, tile_rows, block_rows, here):
    per_block = block_rows // tile_rows
    return pl.multiple_of(
        (here ^ (tile // per_block)) * block_rows + tile % per_block * tile_rows, tile_rows
    )


def forward_kernel(here_ref, q_ref, k_ref, v_ref, *refs, block, tq, tk):
    low_ref, wide_ref, lse_ref, keys = refs[-4:]
    here = here_ref[0]
    seq = q_ref.shape[1]
    keys[...] = k_ref[...].T
    for qi in range(seq // tq):
        q_at = tile_start(qi, tq, block, here)
        query = q_ref[:, pl.ds(q_at, tq)] * 0.125
        peak = total = acc = None
        for ki in range((qi + 1) * tq // tk if tq >= tk else qi * tq // tk + 1):
            k_at = tile_start(ki, tk, block, here)
            scores = jnp.dot(keys[pl.ds(k_at, tk), :], query, preferred_element_type=jnp.float32)
            if (ki + 1) * tk > qi * tq + 1:
                k_pos = ki * tk + lax.broadcasted_iota(jnp.int32, (tk, tq), 0)
                q_pos = qi * tq + lax.broadcasted_iota(jnp.int32, (tk, tq), 1)
                scores = jnp.where(k_pos <= q_pos, scores, masked_score)
            tile_peak = jnp.max(scores, axis=0, keepdims=True)
            new_peak = tile_peak if peak is None else jnp.maximum(peak, tile_peak)
            shifted = jnp.exp(scores - new_peak)
            tile_total = jnp.sum(shifted, axis=0, keepdims=True)
            part = jnp.dot(
                v_ref[:, pl.ds(k_at, tk)], shifted.astype(jnp.bfloat16),
                preferred_element_type=jnp.float32,
            )
            if peak is None:
                total, acc = tile_total, part
            else:
                shrink = jnp.exp(peak - new_peak)
                total = total * shrink + tile_total
                acc = acc * shrink + part
            peak = new_peak
        wide = acc / total
        wide_ref[:, pl.ds(q_at, tq)] = wide
        low_ref[:, pl.ds(q_at, tq)] = wide.astype(jnp.bfloat16)
        lse_ref[0, :, pl.ds(q_at, tq)] = peak + jnp.log(total)


def backward_kernel(
    here_ref, q_ref, k_ref, v_ref, g_ref, wide_ref, lse_ref, *refs, block, tq, tk
):
    out_ref, keys, values, queries, grads, dkeys, dvalues = refs[-7:]
    here = here_ref[0]
    seq = q_ref.shape[1]
    keys[...] = k_ref[...].T
    values[...] = v_ref[...].T
    queries[...] = (q_ref[...] * 0.125).T
    grads[...] = g_ref[...].T
    for qi in range(seq // tq):
        q_at = tile_start(qi, tq, block, here)
        query = q_ref[:, pl.ds(q_at, tq)] * 0.125
        grad = g_ref[:, pl.ds(q_at, tq)]
        query_rows = queries[pl.ds(q_at, tq), :]
        grad_rows = grads[pl.ds(q_at, tq), :]
        lse = lse_ref[0, :, pl.ds(q_at, tq)]
        inner = jnp.sum(
            grad.astype(jnp.float32) * wide_ref[:, pl.ds(q_at, tq)], axis=0, keepdims=True
        )
        acc = None
        for ki in range((qi + 1) * tq // tk if tq >= tk else qi * tq // tk + 1):
            k_at = tile_start(ki, tk, block, here)
            k_rows = pl.ds(k_at, tk)
            scores = jnp.dot(keys[k_rows, :], query, preferred_element_type=jnp.float32)
            probs = jnp.exp(scores - lse)
            if (ki + 1) * tk > qi * tq + 1:
                k_pos = ki * tk + lax.broadcasted_iota(jnp.int32, (tk, tq), 0)
                q_pos = qi * tq + lax.broadcasted_iota(jnp.int32, (tk, tq), 1)
                probs = jnp.where(k_pos <= q_pos, probs, 0.0)
            prob_grad = jnp.dot(values[k_rows, :], grad, preferred_element_type=jnp.float32)
            score_grad = (probs * (prob_grad - inner)).astype(jnp.bfloat16)
            dv = jnp.dot(probs.astype(jnp.bfloat16), grad_rows, preferred_element_type=jnp.float32)
            dk = jnp.dot(score_grad, query_rows, preferred_element_type=jnp.float32)
            dq = jnp.dot(
                k_ref[:, k_rows], score_grad, preferred_element_type=jnp.float32
            )
            acc = dq if acc is None else acc + dq
            if qi * tq // tk * tk <= ki * tk and qi * tq % tk == 0:
                dkeys[k_rows, :] = dk
                dvalues[k_rows, :] = dv
            else:
                dkeys[k_rows, :] += dk
                dvalues[k_rows, :] += dv
        out_ref[:HEAD_DIM, pl.ds(q_at, tq)] = (acc * 0.125).astype(jnp.bfloat16)
    out_ref[HEAD_DIM : 2 * HEAD_DIM, :] = dkeys[...].T.astype(jnp.bfloat16)
    out_ref[2 * HEAD_DIM :, :] = dvalues[...].T.astype(jnp.bfloat16)


def attend_forward(here, qkv, block, first, count, others=(), tq=512, tk=512):
    seq = qkv.shape[1]
    part = lambda j: pl.BlockSpec((HEAD_DIM, seq), lambda h, _: ((first + h) * 3 + j, 0))
    done = pl.BlockSpec((HEAD_DIM, seq), lambda h, _: (h, 0))
    return pl.pallas_call(
        functools.partial(forward_kernel, block=block, tq=tq, tk=tk),
        out_shape=(
            jax.ShapeDtypeStruct((count * HEAD_DIM, seq), jnp.bfloat16),
            jax.ShapeDtypeStruct((count * HEAD_DIM, seq), jnp.float32),
            jax.ShapeDtypeStruct((count, 1, seq), jnp.float32),
        ),
        grid_spec=pltpu.PrefetchScalarGridSpec(
            num_scalar_prefetch=1,
            grid=(count,),
            in_specs=[part(0), part(1), part(2)]
            + [pl.BlockSpec(memory_space=pl.ANY)] * len(others),
            out_specs=(done, done, pl.BlockSpec((1, 1, seq), lambda h, _: (h, 0, 0))),
            scratch_shapes=[pltpu.VMEM((seq, HEAD_DIM), jnp.bfloat16)],
        ),
        compiler_params=pltpu.CompilerParams(vmem_limit_bytes=48 * 2**20),
        cost_estimate=pl.CostEstimate(
            flops=count * seq * seq * 1280, bytes_accessed=count * seq * HEAD_DIM * 12,
            transcendentals=count * seq * seq // 2,
        ),
        name="attn_forward",
    )(here, qkv, qkv, qkv, *others)


def attend_backward(here, qkv, grad, wide, lse, block, others=(), tq=512, tk=512):
    seq = qkv.shape[1]
    heads = grad.shape[0] // HEAD_DIM
    part = lambda j: pl.BlockSpec((HEAD_DIM, seq), lambda h, _: (3 * h + j, 0))
    one = pl.BlockSpec((HEAD_DIM, seq), lambda h, _: (h, 0))
    return pl.pallas_call(
        functools.partial(backward_kernel, block=block, tq=tq, tk=tk),
        out_shape=jax.ShapeDtypeStruct(qkv.shape, jnp.bfloat16),
        grid_spec=pltpu.PrefetchScalarGridSpec(
            num_scalar_prefetch=1,
            grid=(heads,),
            in_specs=[
                part(0), part(1), part(2), one, one,
                pl.BlockSpec((1, 1, seq), lambda h, _: (h, 0, 0)),
            ]
            + [pl.BlockSpec(memory_space=pl.ANY)] * len(others),
            out_specs=pl.BlockSpec((3 * HEAD_DIM, seq), lambda h, _: (h, 0)),
            scratch_shapes=[pltpu.VMEM((seq, HEAD_DIM), jnp.bfloat16)] * 4
            + [pltpu.VMEM((seq, HEAD_DIM), jnp.float32)] * 2,
        ),
        compiler_params=pltpu.CompilerParams(vmem_limit_bytes=48 * 2**20),
        cost_estimate=pl.CostEstimate(
            flops=heads * seq * seq * 1900, bytes_accessed=heads * seq * 64 * 18,
            transcendentals=heads * seq * seq // 2,
        ),
        name="attn_backward",
    )(here, qkv, qkv, qkv, grad, wide, lse, *others)


eps = 1e-05


def layer_norm(rows, gain, shift):
    average = jnp.mean(rows, axis=-1, keepdims=True)
    centred = rows - average
    variance = jnp.mean(centred * centred, axis=-1, keepdims=True)
    return centred * lax.rsqrt(variance + eps) * gain + shift


def gelu_tanh(values):
    return jax.nn.gelu(values, approximate=True)


def swap(value, axis, step):
    count = lax.axis_size(axis)
    return lax.ppermute(value, axis, [(i, i ^ step) for i in range(count)])


def gather_xor(value, axis):
    count = lax.axis_size(axis)
    held = {0: value}
    step = count // 2
    while step:
        held.update({r ^ step: swap(held[r], axis, step) for r in list(held)})
        step //= 2
    return [held[r] for r in range(count)]


def after(value, *others):
    return lax.optimization_barrier((value,) + others)[0]


def once(value, other):
    return value + (other.reshape(-1)[0] * 0).astype(value.dtype)


def gather_row(value, axis):
    index = lax.axis_index("row")
    parts = gather_xor(value, "row")
    if len(parts) == 2:
        low_part = jnp.where(index == 0, parts[0], parts[1])
        high_part = jnp.where(index == 0, parts[1], parts[0])
        return jnp.concatenate([low_part, high_part], axis)
    stacked = jnp.zeros((len(parts),) + value.shape, value.dtype)
    for step, part in enumerate(parts):
        stacked = lax.dynamic_update_index_in_dim(stacked, part, index ^ step, 0)
    shape = list(value.shape)
    shape[axis] *= len(parts)
    return jnp.moveaxis(stacked, 0, axis).reshape(shape)


def send_blocks(stacked, axis):
    index = lax.axis_index(axis)
    own = lax.dynamic_index_in_dim(stacked, index, 0, keepdims=False)
    parts = []
    for step in range(1, stacked.shape[0]):
        part = lax.dynamic_index_in_dim(stacked, index ^ step, 0, keepdims=False)
        parts.append(swap(part.astype(jnp.bfloat16), axis, step))
    return own, parts


def add_up(own, parts):
    total = own.astype(jnp.float32)
    for part in parts:
        total = total + part.astype(jnp.float32)
    return total


def send_total(total, axis):
    total = total.astype(jnp.bfloat16)
    return [total] + [swap(total, axis, s) for s in range(1, lax.axis_size(axis))]


def place(parts, axis):
    index = lax.axis_index(axis)
    out = jnp.zeros((len(parts),) + parts[0].shape, jnp.float32)
    for step, part in enumerate(parts):
        out = lax.dynamic_update_index_in_dim(out, part.astype(jnp.float32), index ^ step, 0)
    return lax.optimization_barrier(out)


def sum_small(value, axes):
    for axis in axes:
        step = 1
        while step < lax.axis_size(axis):
            value = value + swap(value, axis, step)
            step *= 2
    return value


def contract(left, right, left_dim, right_dim):
    return lax.dot_general(
        left, right, (((left_dim,), (right_dim,)), ((), ())), preferred_element_type=jnp.float32
    )


def body(
    inputs,
    pre_attn_gain,
    pre_attn_shift,
    qkv_weight,
    qv_bias,
    out_weight,
    out_bias,
    pre_mlp_gain,
    pre_mlp_shift,
    fc_weight,
    fc_bias,
    proj_weight,
    proj_bias,
    cotangent,
):
    low = jnp.bfloat16
    wide = jnp.float32
    rows, width = inputs.shape
    cols = lax.axis_size("col")
    row_count = lax.axis_size("row")
    row_index = lax.axis_index("row")
    here = lax.axis_index("col").astype(jnp.int32).reshape(1)
    head_cols = qkv_weight.shape[2]
    hidden_cols = fc_weight.shape[1]
    gain_one, shift_one = pre_attn_gain.astype(wide), pre_attn_shift.astype(wide)
    gain_two, shift_two = pre_mlp_gain.astype(wide), pre_mlp_shift.astype(wide)

    heads = head_cols // HEAD_DIM
    dp_count = lax.axis_size("dp")
    stream = inputs.astype(wide)
    normed_one = layer_norm(stream, gain_one, shift_one).astype(low)
    normed = gather_xor(normed_one, "col")
    qkv_own = qkv_weight.reshape(-1, 3, heads, HEAD_DIM).transpose(2, 1, 3, 0)
    qkv_own = qkv_own.reshape(3 * head_cols, -1)
    qkv_full = gather_row(qkv_own, 1)
    bias_wide = qv_bias.astype(wide)
    bias_rows = jnp.stack([bias_wide[0], jnp.zeros_like(bias_wide[0]), bias_wide[1]])
    bias_col = jnp.swapaxes(bias_rows.reshape(3, heads, HEAD_DIM), 0, 1).reshape(-1, 1)
    normed_near = jnp.concatenate(normed[:2], 0)
    normed_far = jnp.concatenate(normed[2:], 0)
    qkv = jnp.concatenate(
        [
            (contract(qkv_full, part, 1, 1) + bias_col).astype(low)
            for part in (normed_near, normed_far)
        ],
        1,
    )
    if row_count == 2:
        inner = proj_weight.shape[0] // 2
        both = swap(
            jnp.concatenate(
                [fc_weight, jnp.concatenate([proj_weight[:inner], proj_weight[inner:]], 1)], 0
            ),
            "row",
            1,
        )
        fc_pair = (fc_weight, both[: fc_weight.shape[0]])
        proj_there = both[fc_weight.shape[0] :]
        proj_there = jnp.concatenate(
            [proj_there[:, : width // 2], proj_there[:, width // 2 :]], 0
        )
        proj_pair = (proj_weight, proj_there)
        fc_full, proj_full = (
            jnp.concatenate(
                [
                    jnp.where(row_index == 0, pair[0], pair[1]),
                    jnp.where(row_index == 0, pair[1], pair[0]),
                ],
                axis,
            )
            for pair, axis in ((fc_pair, 0), (proj_pair, 1))
        )
    else:
        both = fc_full = gather_row(fc_weight, 0)
        proj_full = gather_row(proj_weight, 1)
    cot_far = swap(once(cotangent, normed[2][0, :1]), "col", 2)
    waits = {1: (both,), 2: (cot_far,)}
    attended = [
        attend_forward(here, qkv, rows, head, 1, waits.get(head, ())) for head in range(heads)
    ]
    context_wide = jnp.concatenate([done[1] for done in attended], 0)
    lse = jnp.concatenate([done[2] for done in attended], 0)
    out_near = gather_row(out_weight, 1)
    out_far = gather_row(swap(once(out_weight, attended[0][2][0, 0, :1]), "col", 2), 1)
    out_full = jnp.concatenate(
        [out_near, swap(out_near, "col", 1), out_far, swap(out_far, "col", 1)], 0
    )
    contexts = [
        jnp.concatenate([done[0][:, r * rows : (r + 1) * rows] for done in attended], 0)
        for r in range(cols)
    ]
    contexts = contexts[:1] + [swap(contexts[r], "col", r) for r in range(1, cols)]
    context_own = jnp.concatenate(contexts, 0)
    mid_stream = stream + contract(context_own, out_full, 0, 0) + out_bias.astype(wide)
    normed_two = layer_norm(mid_stream, gain_two, shift_two).astype(low)
    two_far = swap(normed_two, "col", 2)
    fc_bias_wide = fc_bias.astype(wide)

    def forward_and_back(normed_side, cot_side):
        pre_act = contract(normed_side, fc_full, 1, 0) + fc_bias_wide
        hidden_wide, gelu_pull = jax.vjp(gelu_tanh, pre_act)
        hidden = hidden_wide.astype(low)
        return hidden, gelu_pull(contract(cot_side, proj_full, 1, 1))[0].astype(low)

    def weight_parts(hidden, pre_grad, normed_side, cot_side):
        return (
            contract(normed_side, pre_grad, 0, 0),
            contract(cot_side, hidden, 0, 0),
            jnp.sum(pre_grad, axis=0, dtype=wide),
        )

    near_in = jnp.concatenate([normed_two, swap(normed_two, "col", 1)], 0)
    near_cot = jnp.concatenate([cotangent, swap(cotangent, "col", 1)], 0)
    near_hidden, near_grad = forward_and_back(near_in, near_cot)
    near_parts = weight_parts(near_hidden, near_grad, near_in, near_cot)
    near_one = contract(near_grad[rows:], fc_full, 1, 1).astype(low)
    two_here = contract(near_grad[:rows], fc_full, 1, 1) + swap(near_one, "col", 1).astype(wide)
    mlp_one = contract(near_hidden[rows:], proj_full, 1, 0).astype(low)
    mlp_here = contract(near_hidden[:rows], proj_full, 1, 0) + swap(mlp_one, "col", 1).astype(wide)
    two_far, near_parts, two_here = lax.optimization_barrier((two_far, near_parts, two_here))
    far_in = jnp.concatenate([two_far, swap(two_far, "col", 1)], 0)
    far_cot = jnp.concatenate([cot_far, swap(cot_far, "col", 1)], 0)
    far_hidden, far_grad = forward_and_back(far_in, far_cot)
    far_three = contract(far_grad[rows:], fc_full, 1, 1).astype(low)
    far_two = contract(far_grad[:rows], fc_full, 1, 1) + swap(far_three, "col", 1).astype(wide)
    two_there = far_two.astype(low)
    two_back = swap(two_there, "col", 2)
    far_hidden, far_grad, far_in, far_cot = lax.optimization_barrier(
        (far_hidden, far_grad, far_in, far_cot, two_there)
    )[:4]
    far_parts = weight_parts(far_hidden, far_grad, far_in, far_cot)
    fc_own, fc_parts = send_blocks(
        (near_parts[0] + far_parts[0]).reshape(row_count, -1, hidden_cols), "row"
    )
    proj_own, proj_parts = send_blocks(
        (near_parts[1] + far_parts[1]).reshape(row_count, -1, hidden_cols), "row"
    )
    mlp_three = contract(far_hidden[rows:], proj_full, 1, 0).astype(low)
    mlp_two = contract(far_hidden[:rows], proj_full, 1, 0) + swap(mlp_three, "col", 1).astype(wide)
    mlp_there = mlp_two.astype(low)
    qkv_far = gather_row(swap(once(qkv_own, two_back[0, :1]), "col", 2), 1)
    qkv_last = swap(qkv_far, "col", 1)

    normed_two_grad = two_here + two_back.astype(wide)
    out_grad = cotangent.astype(wide)
    norm_two_pull = jax.vjp(layer_norm, mid_stream, gain_two, shift_two)[1]
    stream_two, gain_two_grad, shift_two_grad = norm_two_pull(normed_two_grad)
    mid_grad = out_grad + stream_two
    mid_low = mid_grad.astype(low)
    context_grad_own = contract(out_full, mid_low, 1, 1).astype(low)
    pieces = [context_grad_own[r * head_cols : (r + 1) * head_cols] for r in range(cols)]
    pieces = pieces[:1] + [swap(pieces[r], "col", r) for r in range(1, cols)]
    context_grad = jnp.concatenate(pieces, 1)

    late_low = after(mid_low, context_grad_own)
    out_there = contract(jnp.concatenate([contexts[1], contexts[3]], 0), late_low, 1, 0).astype(low)
    out_recv = swap(out_there, "col", 1)
    fc_own, fc_parts, proj_own, proj_parts = after(
        (fc_own, fc_parts, proj_own, proj_parts), context_grad_own
    )
    mlp_block = jnp.stack(
        [
            add_up(fc_own, fc_parts).reshape(dp_count, -1, hidden_cols),
            add_up(proj_own, proj_parts).reshape(dp_count, -1, hidden_cols),
        ],
        1,
    )
    mlp_own, mlp_slices = send_blocks(mlp_block, "dp")
    small_two = jnp.stack(
        [
            jnp.sum(late_low, axis=0, dtype=wide),
            gain_two_grad,
            shift_two_grad,
            jnp.sum(after(out_grad, context_grad_own), axis=0),
        ]
    )
    out_two = contract(contexts[2], late_low, 1, 0) + out_recv[head_cols:].astype(wide)
    out_back = swap(out_two.astype(low), "col", 2)

    grouped = attend_backward(
        here, qkv, context_grad, context_wide, lse, rows, (out_recv,)
    )
    arrived = [grouped[:, r * rows : (r + 1) * rows] for r in range(cols)]
    arrived = arrived[:1] + [swap(arrived[r], "col", r) for r in range(1, cols)]
    mlp_totals = send_total(add_up(mlp_own, mlp_slices), "dp")
    attn_part = jnp.concatenate(
        [
            contract(grouped[:, : 2 * rows], normed_near, 1, 0)
            + contract(grouped[:, 2 * rows :], normed_far, 1, 0),
            contract(contexts[0], late_low, 1, 0)
            + out_recv[:head_cols].astype(wide)
            + out_back.astype(wide),
        ],
        0,
    )
    if row_count == 2:
        half = width // 2
        attn_own = jnp.where(row_index == 0, attn_part[:, :half], attn_part[:, half:])
        sent = jnp.where(row_index == 0, attn_part[:, half:], attn_part[:, :half])
        attn_parts = [swap(sent.astype(low), "row", 1)]
    else:
        attn_blocks = jnp.moveaxis(attn_part.reshape(attn_part.shape[0], row_count, -1), 1, 0)
        attn_own, attn_parts = send_blocks(attn_blocks, "row")
    qkv_all = [qkv_full, swap(qkv_full, "col", 1), qkv_far, qkv_last]
    normed_one_grad = contract(
        jnp.concatenate(arrived, 0), jnp.concatenate(qkv_all, 0), 0, 0
    )
    attn_block = add_up(attn_own, attn_parts).reshape(dp_count, -1, attn_own.shape[1])
    attn_own, attn_slices = send_blocks(attn_block, "dp")
    norm_one_pull = jax.vjp(layer_norm, stream, gain_one, shift_one)[1]
    stream_one, gain_one_grad, shift_one_grad = norm_one_pull(normed_one_grad)
    input_grad = (mid_grad + stream_one).astype(low)
    small = jnp.concatenate([jnp.stack([gain_one_grad, shift_one_grad]), small_two], 0)
    small = sum_small(small, ("col",))
    qv_part = jnp.sum(grouped.astype(wide), axis=1).reshape(heads, 3, HEAD_DIM)
    qv_part = jnp.swapaxes(qv_part, 0, 1)[0::2].reshape(-1)
    extra = jnp.concatenate([qv_part, near_parts[2] + far_parts[2]])
    extra = jnp.pad(extra, (0, -extra.shape[0] % width)).reshape(-1, width)
    small = sum_small(jnp.concatenate([small, extra], 0), ("row", "dp"))
    extra = small[6:].reshape(-1)
    attn_sum = place(send_total(add_up(attn_own, attn_slices), "dp"), "dp")
    attn_sum = attn_sum.reshape(-1, attn_own.shape[1])
    qkv_sum = attn_sum[: 3 * head_cols].reshape(heads, 3, HEAD_DIM, -1)
    mlp_sums = place(mlp_totals, "dp")
    mlp_back = swap(after(mlp_there, arrived[2]), "col", 2)
    block_out = mid_stream + mlp_here + mlp_back.astype(wide) + proj_bias.astype(wide)
    return (
        block_out.astype(low),
        input_grad,
        small[0],
        small[1],
        qkv_sum.transpose(3, 1, 0, 2).reshape(qkv_weight.shape),
        extra[: 2 * head_cols].reshape(2, head_cols),
        attn_sum[3 * head_cols :],
        small[2],
        small[3],
        small[4],
        mlp_sums[:, 0].reshape(fc_weight.shape),
        extra[2 * head_cols : 2 * head_cols + hidden_cols],
        mlp_sums[:, 1].reshape(-1, hidden_cols).T,
        small[5],
    )


def solution(mesh):
    placed = (
        P(("dp", "row", "col"), None),
        P(),
        P(),
        P("row", None, "col"),
        P(None, "col"),
        P("col", "row"),
        P(),
        P(),
        P(),
        P("row", "col"),
        P("col"),
        P("col", "row"),
        P(),
        P(("dp", "row", "col"), None),
    )
    return jax.shard_map(
        body,
        mesh=mesh,
        in_specs=placed,
        out_specs=(
            P(("dp", "row", "col"), None),
            P(("dp", "row", "col"), None),
            P(),
            P(),
            P("row", None, "col"),
            P(None, "col"),
            P("col", "row"),
            P(),
            P(),
            P(),
            P("row", "col"),
            P("col"),
            P("col", "row"),
            P(),
        ),
        check_vma=False,
    )
```

```python
import functools
import jax
import jax.numpy as jnp
from jax import lax
from jax.experimental import pallas as pl
from jax.experimental.pallas import tpu as pltpu
from jax.sharding import PartitionSpec as P

HEAD_DIM = 64
masked_score = -1e30


def tile_start(tile, tile_rows, block_rows, here):
    per_block = block_rows // tile_rows
    return pl.multiple_of(
        (here ^ (tile // per_block)) * block_rows + tile % per_block * tile_rows, tile_rows
    )


def forward_kernel(here_ref, q_ref, k_ref, v_ref, *refs, block, tq, tk):
    low_ref, wide_ref, lse_ref, keys = refs[-4:]
    here = here_ref[0]
    seq = q_ref.shape[1]
    keys[...] = k_ref[...].T
    for qi in range(seq // tq):
        q_at = tile_start(qi, tq, block, here)
        query = q_ref[:, pl.ds(q_at, tq)] * 0.125
        peak = total = acc = None
        for ki in range((qi + 1) * tq // tk if tq >= tk else qi * tq // tk + 1):
            k_at = tile_start(ki, tk, block, here)
            scores = jnp.dot(keys[pl.ds(k_at, tk), :], query, preferred_element_type=jnp.float32)
            if (ki + 1) * tk > qi * tq + 1:
                k_pos = ki * tk + lax.broadcasted_iota(jnp.int32, (tk, tq), 0)
                q_pos = qi * tq + lax.broadcasted_iota(jnp.int32, (tk, tq), 1)
                scores = jnp.where(k_pos <= q_pos, scores, masked_score)
            tile_peak = jnp.max(scores, axis=0, keepdims=True)
            new_peak = tile_peak if peak is None else jnp.maximum(peak, tile_peak)
            shifted = jnp.exp(scores - new_peak)
            tile_total = jnp.sum(shifted, axis=0, keepdims=True)
            part = jnp.dot(
                v_ref[:, pl.ds(k_at, tk)], shifted.astype(jnp.bfloat16),
                preferred_element_type=jnp.float32,
            )
            if peak is None:
                total, acc = tile_total, part
            else:
                shrink = jnp.exp(peak - new_peak)
                total = total * shrink + tile_total
                acc = acc * shrink + part
            peak = new_peak
        wide = acc / total
        wide_ref[:, pl.ds(q_at, tq)] = wide
        low_ref[:, pl.ds(q_at, tq)] = wide.astype(jnp.bfloat16)
        lse_ref[0, :, pl.ds(q_at, tq)] = peak + jnp.log(total)


def backward_kernel(
    here_ref, q_ref, k_ref, v_ref, g_ref, wide_ref, lse_ref, *refs, block, tq, tk
):
    out_ref, keys, values, queries, grads, dkeys, dvalues = refs[-7:]
    here = here_ref[0]
    seq = q_ref.shape[1]
    keys[...] = k_ref[...].T
    values[...] = v_ref[...].T
    queries[...] = (q_ref[...] * 0.125).T
    grads[...] = g_ref[...].T
    for qi in range(seq // tq):
        q_at = tile_start(qi, tq, block, here)
        query = q_ref[:, pl.ds(q_at, tq)] * 0.125
        grad = g_ref[:, pl.ds(q_at, tq)]
        query_rows = queries[pl.ds(q_at, tq), :]
        grad_rows = grads[pl.ds(q_at, tq), :]
        lse = lse_ref[0, :, pl.ds(q_at, tq)]
        inner = jnp.sum(
            grad.astype(jnp.float32) * wide_ref[:, pl.ds(q_at, tq)], axis=0, keepdims=True
        )
        acc = None
        for ki in range((qi + 1) * tq // tk if tq >= tk else qi * tq // tk + 1):
            k_at = tile_start(ki, tk, block, here)
            k_rows = pl.ds(k_at, tk)
            scores = jnp.dot(keys[k_rows, :], query, preferred_element_type=jnp.float32)
            probs = jnp.exp(scores - lse)
            if (ki + 1) * tk > qi * tq + 1:
                k_pos = ki * tk + lax.broadcasted_iota(jnp.int32, (tk, tq), 0)
                q_pos = qi * tq + lax.broadcasted_iota(jnp.int32, (tk, tq), 1)
                probs = jnp.where(k_pos <= q_pos, probs, 0.0)
            prob_grad = jnp.dot(values[k_rows, :], grad, preferred_element_type=jnp.float32)
            score_grad = (probs * (prob_grad - inner)).astype(jnp.bfloat16)
            dv = jnp.dot(probs.astype(jnp.bfloat16), grad_rows, preferred_element_type=jnp.float32)
            dk = jnp.dot(score_grad, query_rows, preferred_element_type=jnp.float32)
            dq = jnp.dot(
                k_ref[:, k_rows], score_grad, preferred_element_type=jnp.float32
            )
            acc = dq if acc is None else acc + dq
            if qi * tq // tk * tk <= ki * tk and qi * tq % tk == 0:
                dkeys[k_rows, :] = dk
                dvalues[k_rows, :] = dv
            else:
                dkeys[k_rows, :] += dk
                dvalues[k_rows, :] += dv
        out_ref[:HEAD_DIM, pl.ds(q_at, tq)] = (acc * 0.125).astype(jnp.bfloat16)
    out_ref[HEAD_DIM : 2 * HEAD_DIM, :] = dkeys[...].T.astype(jnp.bfloat16)
    out_ref[2 * HEAD_DIM :, :] = dvalues[...].T.astype(jnp.bfloat16)


def attend_forward(here, qkv, block, first, count, others=(), tq=512, tk=512):
    seq = qkv.shape[1]
    part = lambda j: pl.BlockSpec((HEAD_DIM, seq), lambda h, _: ((first + h) * 3 + j, 0))
    done = pl.BlockSpec((HEAD_DIM, seq), lambda h, _: (h, 0))
    return pl.pallas_call(
        functools.partial(forward_kernel, block=block, tq=tq, tk=tk),
        out_shape=(
            jax.ShapeDtypeStruct((count * HEAD_DIM, seq), jnp.bfloat16),
            jax.ShapeDtypeStruct((count * HEAD_DIM, seq), jnp.float32),
            jax.ShapeDtypeStruct((count, 1, seq), jnp.float32),
        ),
        grid_spec=pltpu.PrefetchScalarGridSpec(
            num_scalar_prefetch=1,
            grid=(count,),
            in_specs=[part(0), part(1), part(2)]
            + [pl.BlockSpec(memory_space=pl.ANY)] * len(others),
            out_specs=(done, done, pl.BlockSpec((1, 1, seq), lambda h, _: (h, 0, 0))),
            scratch_shapes=[pltpu.VMEM((seq, HEAD_DIM), jnp.bfloat16)],
        ),
        compiler_params=pltpu.CompilerParams(vmem_limit_bytes=48 * 2**20),
        cost_estimate=pl.CostEstimate(
            flops=count * seq * seq * 1280, bytes_accessed=count * seq * HEAD_DIM * 12,
            transcendentals=count * seq * seq // 2,
        ),
        name="attn_forward",
    )(here, qkv, qkv, qkv, *others)


def attend_backward(here, qkv, grad, wide, lse, block, others=(), tq=512, tk=512):
    seq = qkv.shape[1]
    heads = grad.shape[0] // HEAD_DIM
    part = lambda j: pl.BlockSpec((HEAD_DIM, seq), lambda h, _: (3 * h + j, 0))
    one = pl.BlockSpec((HEAD_DIM, seq), lambda h, _: (h, 0))
    return pl.pallas_call(
        functools.partial(backward_kernel, block=block, tq=tq, tk=tk),
        out_shape=jax.ShapeDtypeStruct(qkv.shape, jnp.bfloat16),
        grid_spec=pltpu.PrefetchScalarGridSpec(
            num_scalar_prefetch=1,
            grid=(heads,),
            in_specs=[
                part(0), part(1), part(2), one, one,
                pl.BlockSpec((1, 1, seq), lambda h, _: (h, 0, 0)),
            ]
            + [pl.BlockSpec(memory_space=pl.ANY)] * len(others),
            out_specs=pl.BlockSpec((3 * HEAD_DIM, seq), lambda h, _: (h, 0)),
            scratch_shapes=[pltpu.VMEM((seq, HEAD_DIM), jnp.bfloat16)] * 4
            + [pltpu.VMEM((seq, HEAD_DIM), jnp.float32)] * 2,
        ),
        compiler_params=pltpu.CompilerParams(vmem_limit_bytes=48 * 2**20),
        cost_estimate=pl.CostEstimate(
            flops=heads * seq * seq * 1900, bytes_accessed=heads * seq * 64 * 18,
            transcendentals=heads * seq * seq // 2,
        ),
        name="attn_backward",
    )(here, qkv, qkv, qkv, grad, wide, lse, *others)


eps = 1e-05


def layer_norm(rows, gain, shift):
    average = jnp.mean(rows, axis=-1, keepdims=True)
    centred = rows - average
    variance = jnp.mean(centred * centred, axis=-1, keepdims=True)
    return centred * lax.rsqrt(variance + eps) * gain + shift


def gelu_tanh(values):
    return jax.nn.gelu(values, approximate=True)


def swap(value, axis, step):
    count = lax.axis_size(axis)
    return lax.ppermute(value, axis, [(i, i ^ step) for i in range(count)])


def gather_xor(value, axis):
    count = lax.axis_size(axis)
    held = {0: value}
    step = count // 2
    while step:
        held.update({r ^ step: swap(held[r], axis, step) for r in list(held)})
        step //= 2
    return [held[r] for r in range(count)]


def after(value, *others):
    return lax.optimization_barrier((value,) + others)[0]


def once(value, other):
    return value + (other.reshape(-1)[0] * 0).astype(value.dtype)


def gather_row(value, axis):
    index = lax.axis_index("row")
    parts = gather_xor(value, "row")
    if len(parts) == 2:
        low_part = jnp.where(index == 0, parts[0], parts[1])
        high_part = jnp.where(index == 0, parts[1], parts[0])
        return jnp.concatenate([low_part, high_part], axis)
    stacked = jnp.zeros((len(parts),) + value.shape, value.dtype)
    for step, part in enumerate(parts):
        stacked = lax.dynamic_update_index_in_dim(stacked, part, index ^ step, 0)
    shape = list(value.shape)
    shape[axis] *= len(parts)
    return jnp.moveaxis(stacked, 0, axis).reshape(shape)


def send_blocks(stacked, axis):
    index = lax.axis_index(axis)
    own = lax.dynamic_index_in_dim(stacked, index, 0, keepdims=False)
    parts = []
    for step in range(1, stacked.shape[0]):
        part = lax.dynamic_index_in_dim(stacked, index ^ step, 0, keepdims=False)
        parts.append(swap(part.astype(jnp.bfloat16), axis, step))
    return own, parts


def add_up(own, parts):
    total = own.astype(jnp.float32)
    for part in parts:
        total = total + part.astype(jnp.float32)
    return total


def send_total(total, axis):
    total = total.astype(jnp.bfloat16)
    return [total] + [swap(total, axis, s) for s in range(1, lax.axis_size(axis))]


def place(parts, axis):
    index = lax.axis_index(axis)
    out = jnp.zeros((len(parts),) + parts[0].shape, jnp.float32)
    for step, part in enumerate(parts):
        out = lax.dynamic_update_index_in_dim(out, part.astype(jnp.float32), index ^ step, 0)
    return lax.optimization_barrier(out)


def sum_small(value, axes):
    for axis in axes:
        step = 1
        while step < lax.axis_size(axis):
            value = value + swap(value, axis, step)
            step *= 2
    return value


def contract(left, right, left_dim, right_dim):
    return lax.dot_general(
        left, right, (((left_dim,), (right_dim,)), ((), ())), preferred_element_type=jnp.float32
    )


def body(
    inputs,
    pre_attn_gain,
    pre_attn_shift,
    qkv_weight,
    qv_bias,
    out_weight,
    out_bias,
    pre_mlp_gain,
    pre_mlp_shift,
    fc_weight,
    fc_bias,
    proj_weight,
    proj_bias,
    cotangent,
):
    low = jnp.bfloat16
    wide = jnp.float32
    rows, width = inputs.shape
    cols = lax.axis_size("col")
    row_count = lax.axis_size("row")
    row_index = lax.axis_index("row")
    here = lax.axis_index("col").astype(jnp.int32).reshape(1)
    head_cols = qkv_weight.shape[2]
    hidden_cols = fc_weight.shape[1]
    gain_one, shift_one = pre_attn_gain.astype(wide), pre_attn_shift.astype(wide)
    gain_two, shift_two = pre_mlp_gain.astype(wide), pre_mlp_shift.astype(wide)

    heads = head_cols // HEAD_DIM
    dp_count = lax.axis_size("dp")
    stream = inputs.astype(wide)
    normed_one = layer_norm(stream, gain_one, shift_one).astype(low)
    normed = gather_xor(normed_one, "col")
    qkv_own = qkv_weight.reshape(-1, 3, heads, HEAD_DIM).transpose(2, 1, 3, 0)
    qkv_own = qkv_own.reshape(3 * head_cols, -1)
    qkv_full = gather_row(qkv_own, 1)
    bias_wide = qv_bias.astype(wide)
    bias_rows = jnp.stack([bias_wide[0], jnp.zeros_like(bias_wide[0]), bias_wide[1]])
    bias_col = jnp.swapaxes(bias_rows.reshape(3, heads, HEAD_DIM), 0, 1).reshape(-1, 1)
    normed_near = jnp.concatenate(normed[:2], 0)
    normed_far = jnp.concatenate(normed[2:], 0)
    qkv = jnp.concatenate(
        [
            (contract(qkv_full, part, 1, 1) + bias_col).astype(low)
            for part in (normed_near, normed_far)
        ],
        1,
    )
    if row_count == 2:
        inner = proj_weight.shape[0] // 2
        both = swap(
            jnp.concatenate(
                [fc_weight, jnp.concatenate([proj_weight[:inner], proj_weight[inner:]], 1)], 0
            ),
            "row",
            1,
        )
        fc_pair = (fc_weight, both[: fc_weight.shape[0]])
        proj_there = both[fc_weight.shape[0] :]
        proj_there = jnp.concatenate(
            [proj_there[:, : width // 2], proj_there[:, width // 2 :]], 0
        )
        proj_pair = (proj_weight, proj_there)
        fc_full, proj_full = (
            jnp.concatenate(
                [
                    jnp.where(row_index == 0, pair[0], pair[1]),
                    jnp.where(row_index == 0, pair[1], pair[0]),
                ],
                axis,
            )
            for pair, axis in ((fc_pair, 0), (proj_pair, 1))
        )
    else:
        both = fc_full = gather_row(fc_weight, 0)
        proj_full = gather_row(proj_weight, 1)
    cot_far = swap(once(cotangent, normed[2][0, :1]), "col", 2)
    waits = {1: (both,), 2: (cot_far,)}
    attended = [
        attend_forward(here, qkv, rows, head, 1, waits.get(head, ())) for head in range(heads)
    ]
    context_wide = jnp.concatenate([done[1] for done in attended], 0)
    lse = jnp.concatenate([done[2] for done in attended], 0)
    out_near = gather_row(out_weight, 1)
    out_far = gather_row(swap(once(out_weight, attended[0][2][0, 0, :1]), "col", 2), 1)
    out_full = jnp.concatenate(
        [out_near, swap(out_near, "col", 1), out_far, swap(out_far, "col", 1)], 0
    )
    contexts = [
        jnp.concatenate([done[0][:, r * rows : (r + 1) * rows] for done in attended], 0)
        for r in range(cols)
    ]
    contexts = contexts[:1] + [swap(contexts[r], "col", r) for r in range(1, cols)]
    context_own = jnp.concatenate(contexts, 0)
    mid_stream = stream + contract(context_own, out_full, 0, 0) + out_bias.astype(wide)
    normed_two = layer_norm(mid_stream, gain_two, shift_two).astype(low)
    two_far = swap(normed_two, "col", 2)
    fc_bias_wide = fc_bias.astype(wide)

    def forward_and_back(normed_side, cot_side):
        pre_act = contract(normed_side, fc_full, 1, 0) + fc_bias_wide
        hidden_wide, gelu_pull = jax.vjp(gelu_tanh, pre_act)
        hidden = hidden_wide.astype(low)
        return hidden, gelu_pull(contract(cot_side, proj_full, 1, 1))[0].astype(low)

    def weight_parts(hidden, pre_grad, normed_side, cot_side):
        return (
            contract(normed_side, pre_grad, 0, 0),
            contract(cot_side, hidden, 0, 0),
            jnp.sum(pre_grad, axis=0, dtype=wide),
        )

    near_in = jnp.concatenate([normed_two, swap(normed_two, "col", 1)], 0)
    near_cot = jnp.concatenate([cotangent, swap(cotangent, "col", 1)], 0)
    near_hidden, near_grad = forward_and_back(near_in, near_cot)
    near_one = contract(near_grad[rows:], fc_full, 1, 1).astype(low)
    two_here = contract(near_grad[:rows], fc_full, 1, 1) + swap(near_one, "col", 1).astype(wide)
    mlp_one = contract(near_hidden[rows:], proj_full, 1, 0).astype(low)
    mlp_here = contract(near_hidden[:rows], proj_full, 1, 0) + swap(mlp_one, "col", 1).astype(wide)
    two_far = once(two_far, near_one[0, :1])
    far_in = jnp.concatenate([two_far, swap(two_far, "col", 1)], 0)
    far_cot = jnp.concatenate([cot_far, swap(cot_far, "col", 1)], 0)
    far_hidden, far_grad = forward_and_back(far_in, far_cot)
    far_three = contract(far_grad[rows:], fc_full, 1, 1).astype(low)
    far_two = contract(far_grad[:rows], fc_full, 1, 1) + swap(far_three, "col", 1).astype(wide)
    two_there = far_two.astype(low)
    two_back = swap(two_there, "col", 2)
    near_parts = weight_parts(
        once(near_hidden, two_there[0, :1]), once(near_grad, two_there[0, :1]), near_in, near_cot
    )
    far_parts = weight_parts(far_hidden, far_grad, far_in, far_cot)
    fc_own, fc_parts = send_blocks(
        (near_parts[0] + far_parts[0]).reshape(row_count, -1, hidden_cols), "row"
    )
    proj_own, proj_parts = send_blocks(
        (near_parts[1] + far_parts[1]).reshape(row_count, -1, hidden_cols), "row"
    )
    mlp_three = contract(far_hidden[rows:], proj_full, 1, 0).astype(low)
    mlp_two = contract(far_hidden[:rows], proj_full, 1, 0) + swap(mlp_three, "col", 1).astype(wide)
    mlp_there = mlp_two.astype(low)
    qkv_far = swap(once(qkv_full, two_back[0, :1]), "col", 2)
    qkv_beside = swap(qkv_full, "col", 1)

    normed_two_grad = two_here + two_back.astype(wide)
    out_grad = cotangent.astype(wide)
    norm_two_pull = jax.vjp(layer_norm, mid_stream, gain_two, shift_two)[1]
    stream_two, gain_two_grad, shift_two_grad = norm_two_pull(normed_two_grad)
    mid_grad = out_grad + stream_two
    mid_low = mid_grad.astype(low)
    context_grad_own = contract(out_full, mid_low, 1, 1).astype(low)
    pieces = [context_grad_own[r * head_cols : (r + 1) * head_cols] for r in range(cols)]
    pieces = pieces[:1] + [swap(pieces[r], "col", r) for r in range(1, cols)]
    context_grad = jnp.concatenate(pieces, 1)

    late_low = after(mid_low, context_grad_own)
    out_there = contract(jnp.concatenate([contexts[1], contexts[3]], 0), late_low, 1, 0).astype(low)
    out_recv = swap(out_there, "col", 1)
    fc_own, proj_own = (once(own, context_grad_own[0, :1]) for own in (fc_own, proj_own))
    mlp_block = jnp.stack(
        [
            add_up(fc_own, fc_parts).reshape(dp_count, -1, hidden_cols),
            add_up(proj_own, proj_parts).reshape(dp_count, -1, hidden_cols),
        ],
        1,
    )
    mlp_own, mlp_slices = send_blocks(mlp_block, "dp")
    small_two = jnp.stack(
        [
            jnp.sum(late_low, axis=0, dtype=wide),
            gain_two_grad,
            shift_two_grad,
            jnp.sum(after(out_grad, context_grad_own), axis=0),
        ]
    )
    out_two = contract(contexts[2], late_low, 1, 0) + out_recv[head_cols:].astype(wide)
    out_back = swap(out_two.astype(low), "col", 2)

    grouped = attend_backward(
        here, qkv, context_grad, context_wide, lse, rows, (out_recv, qkv_beside)
    )
    arrived = [grouped[:, r * rows : (r + 1) * rows] for r in range(cols)]
    arrived = arrived[:1] + [swap(arrived[r], "col", r) for r in range(1, cols)]
    mlp_totals = send_total(add_up(once(mlp_own, grouped[0, :1]), mlp_slices), "dp")
    attn_part = jnp.concatenate(
        [
            contract(grouped[:, : 2 * rows], normed_near, 1, 0)
            + contract(grouped[:, 2 * rows :], normed_far, 1, 0),
            contract(contexts[0], late_low, 1, 0)
            + out_recv[:head_cols].astype(wide)
            + out_back.astype(wide),
        ],
        0,
    )
    if row_count == 2:
        half = width // 2
        attn_own = jnp.where(row_index == 0, attn_part[:, :half], attn_part[:, half:])
        sent = jnp.where(row_index == 0, attn_part[:, half:], attn_part[:, :half])
        attn_parts = [swap(sent.astype(low), "row", 1)]
    else:
        attn_blocks = jnp.moveaxis(attn_part.reshape(attn_part.shape[0], row_count, -1), 1, 0)
        attn_own, attn_parts = send_blocks(attn_blocks, "row")
    qkv_all = [qkv_full, qkv_beside, qkv_far, swap(qkv_far, "col", 1)]
    normed_one_grad = contract(
        jnp.concatenate(arrived, 0), jnp.concatenate(qkv_all, 0), 0, 0
    )
    attn_block = add_up(attn_own, attn_parts).reshape(dp_count, -1, attn_own.shape[1])
    attn_own, attn_slices = send_blocks(attn_block, "dp")
    norm_one_pull = jax.vjp(layer_norm, stream, gain_one, shift_one)[1]
    stream_one, gain_one_grad, shift_one_grad = norm_one_pull(normed_one_grad)
    input_grad = (mid_grad + stream_one).astype(low)
    small = jnp.concatenate([jnp.stack([gain_one_grad, shift_one_grad]), small_two], 0)
    small = sum_small(small, ("col",))
    qv_part = jnp.sum(grouped.astype(wide), axis=1).reshape(heads, 3, HEAD_DIM)
    qv_part = jnp.swapaxes(qv_part, 0, 1)[0::2].reshape(-1)
    extra = jnp.concatenate([qv_part, near_parts[2] + far_parts[2]])
    extra = jnp.pad(extra, (0, -extra.shape[0] % width)).reshape(-1, width)
    small = sum_small(jnp.concatenate([small, extra], 0), ("row", "dp"))
    extra = small[6:].reshape(-1)
    attn_sum = place(send_total(add_up(attn_own, attn_slices), "dp"), "dp")
    attn_sum = attn_sum.reshape(-1, attn_own.shape[1])
    qkv_sum = attn_sum[: 3 * head_cols].reshape(heads, 3, HEAD_DIM, -1)
    mlp_sums = place(mlp_totals, "dp")
    mlp_back = swap(after(mlp_there, arrived[2]), "col", 2)
    block_out = mid_stream + mlp_here + mlp_back.astype(wide) + proj_bias.astype(wide)
    return (
        block_out.astype(low),
        input_grad,
        small[0],
        small[1],
        qkv_sum.transpose(3, 1, 0, 2).reshape(qkv_weight.shape),
        extra[: 2 * head_cols].reshape(2, head_cols),
        attn_sum[3 * head_cols :],
        small[2],
        small[3],
        small[4],
        mlp_sums[:, 0].reshape(fc_weight.shape),
        extra[2 * head_cols : 2 * head_cols + hidden_cols],
        mlp_sums[:, 1].reshape(-1, hidden_cols).T,
        small[5],
    )


def solution(mesh):
    placed = (
        P(("dp", "row", "col"), None),
        P(),
        P(),
        P("row", None, "col"),
        P(None, "col"),
        P("col", "row"),
        P(),
        P(),
        P(),
        P("row", "col"),
        P("col"),
        P("col", "row"),
        P(),
        P(("dp", "row", "col"), None),
    )
    return jax.shard_map(
        body,
        mesh=mesh,
        in_specs=placed,
        out_specs=(
            P(("dp", "row", "col"), None),
            P(("dp", "row", "col"), None),
            P(),
            P(),
            P("row", None, "col"),
            P(None, "col"),
            P("col", "row"),
            P(),
            P(),
            P(),
            P("row", "col"),
            P("col"),
            P("col", "row"),
            P(),
        ),
        check_vma=False,
    )
```

```python
import functools
import jax
import jax.numpy as jnp
from jax import lax
from jax.experimental import pallas as pl
from jax.experimental.pallas import tpu as pltpu
from jax.sharding import PartitionSpec as P

HEAD_DIM = 64
masked_score = -1e30


def tile_start(tile, tile_rows, block_rows, here):
    per_block = block_rows // tile_rows
    return pl.multiple_of(
        (here ^ (tile // per_block)) * block_rows + tile % per_block * tile_rows, tile_rows
    )


def forward_kernel(here_ref, q_ref, k_ref, v_ref, *refs, block, tq, tk):
    low_ref, wide_ref, lse_ref, keys = refs[-4:]
    here = here_ref[0]
    seq = q_ref.shape[1]
    keys[...] = k_ref[...].T
    for qi in range(seq // tq):
        q_at = tile_start(qi, tq, block, here)
        query = q_ref[:, pl.ds(q_at, tq)] * 0.125
        peak = total = acc = None
        for ki in range((qi + 1) * tq // tk if tq >= tk else qi * tq // tk + 1):
            k_at = tile_start(ki, tk, block, here)
            scores = jnp.dot(keys[pl.ds(k_at, tk), :], query, preferred_element_type=jnp.float32)
            if (ki + 1) * tk > qi * tq + 1:
                k_pos = ki * tk + lax.broadcasted_iota(jnp.int32, (tk, tq), 0)
                q_pos = qi * tq + lax.broadcasted_iota(jnp.int32, (tk, tq), 1)
                scores = jnp.where(k_pos <= q_pos, scores, masked_score)
            tile_peak = jnp.max(scores, axis=0, keepdims=True)
            new_peak = tile_peak if peak is None else jnp.maximum(peak, tile_peak)
            shifted = jnp.exp(scores - new_peak)
            tile_total = jnp.sum(shifted, axis=0, keepdims=True)
            part = jnp.dot(
                v_ref[:, pl.ds(k_at, tk)], shifted.astype(jnp.bfloat16),
                preferred_element_type=jnp.float32,
            )
            if peak is None:
                total, acc = tile_total, part
            else:
                shrink = jnp.exp(peak - new_peak)
                total = total * shrink + tile_total
                acc = acc * shrink + part
            peak = new_peak
        wide = acc / total
        wide_ref[:, pl.ds(q_at, tq)] = wide
        low_ref[:, pl.ds(q_at, tq)] = wide.astype(jnp.bfloat16)
        lse_ref[0, :, pl.ds(q_at, tq)] = peak + jnp.log(total)


def backward_kernel(
    here_ref, q_ref, k_ref, v_ref, g_ref, wide_ref, lse_ref, *refs, block, tq, tk
):
    out_ref, keys, values, queries, grads, dkeys, dvalues = refs[-7:]
    here = here_ref[0]
    seq = q_ref.shape[1]
    keys[...] = k_ref[...].T
    values[...] = v_ref[...].T
    queries[...] = (q_ref[...] * 0.125).T
    grads[...] = g_ref[...].T
    for qi in range(seq // tq):
        q_at = tile_start(qi, tq, block, here)
        query = q_ref[:, pl.ds(q_at, tq)] * 0.125
        grad = g_ref[:, pl.ds(q_at, tq)]
        query_rows = queries[pl.ds(q_at, tq), :]
        grad_rows = grads[pl.ds(q_at, tq), :]
        lse = lse_ref[0, :, pl.ds(q_at, tq)]
        inner = jnp.sum(
            grad.astype(jnp.float32) * wide_ref[:, pl.ds(q_at, tq)], axis=0, keepdims=True
        )
        acc = None
        for ki in range((qi + 1) * tq // tk if tq >= tk else qi * tq // tk + 1):
            k_at = tile_start(ki, tk, block, here)
            k_rows = pl.ds(k_at, tk)
            scores = jnp.dot(keys[k_rows, :], query, preferred_element_type=jnp.float32)
            probs = jnp.exp(scores - lse)
            if (ki + 1) * tk > qi * tq + 1:
                k_pos = ki * tk + lax.broadcasted_iota(jnp.int32, (tk, tq), 0)
                q_pos = qi * tq + lax.broadcasted_iota(jnp.int32, (tk, tq), 1)
                probs = jnp.where(k_pos <= q_pos, probs, 0.0)
            prob_grad = jnp.dot(values[k_rows, :], grad, preferred_element_type=jnp.float32)
            score_grad = (probs * (prob_grad - inner)).astype(jnp.bfloat16)
            dv = jnp.dot(probs.astype(jnp.bfloat16), grad_rows, preferred_element_type=jnp.float32)
            dk = jnp.dot(score_grad, query_rows, preferred_element_type=jnp.float32)
            dq = jnp.dot(
                k_ref[:, k_rows], score_grad, preferred_element_type=jnp.float32
            )
            acc = dq if acc is None else acc + dq
            if qi * tq // tk * tk <= ki * tk and qi * tq % tk == 0:
                dkeys[k_rows, :] = dk
                dvalues[k_rows, :] = dv
            else:
                dkeys[k_rows, :] += dk
                dvalues[k_rows, :] += dv
        out_ref[:HEAD_DIM, pl.ds(q_at, tq)] = (acc * 0.125).astype(jnp.bfloat16)
    out_ref[HEAD_DIM : 2 * HEAD_DIM, :] = dkeys[...].T.astype(jnp.bfloat16)
    out_ref[2 * HEAD_DIM :, :] = dvalues[...].T.astype(jnp.bfloat16)


def attend_forward(here, qkv, block, first, count, others=(), tq=512, tk=512):
    seq = qkv.shape[1]
    part = lambda j: pl.BlockSpec((HEAD_DIM, seq), lambda h, _: ((first + h) * 3 + j, 0))
    done = pl.BlockSpec((HEAD_DIM, seq), lambda h, _: (h, 0))
    return pl.pallas_call(
        functools.partial(forward_kernel, block=block, tq=tq, tk=tk),
        out_shape=(
            jax.ShapeDtypeStruct((count * HEAD_DIM, seq), jnp.bfloat16),
            jax.ShapeDtypeStruct((count * HEAD_DIM, seq), jnp.float32),
            jax.ShapeDtypeStruct((count, 1, seq), jnp.float32),
        ),
        grid_spec=pltpu.PrefetchScalarGridSpec(
            num_scalar_prefetch=1,
            grid=(count,),
            in_specs=[part(0), part(1), part(2)]
            + [pl.BlockSpec(memory_space=pl.ANY)] * len(others),
            out_specs=(done, done, pl.BlockSpec((1, 1, seq), lambda h, _: (h, 0, 0))),
            scratch_shapes=[pltpu.VMEM((seq, HEAD_DIM), jnp.bfloat16)],
        ),
        compiler_params=pltpu.CompilerParams(vmem_limit_bytes=48 * 2**20),
        cost_estimate=pl.CostEstimate(
            flops=count * seq * seq * 1280, bytes_accessed=count * seq * HEAD_DIM * 12,
            transcendentals=count * seq * seq // 2,
        ),
        name="attn_forward",
    )(here, qkv, qkv, qkv, *others)


def attend_backward(here, qkv, grad, wide, lse, block, others=(), tq=512, tk=512):
    seq = qkv.shape[1]
    heads = grad.shape[0] // HEAD_DIM
    part = lambda j: pl.BlockSpec((HEAD_DIM, seq), lambda h, _: (3 * h + j, 0))
    one = pl.BlockSpec((HEAD_DIM, seq), lambda h, _: (h, 0))
    return pl.pallas_call(
        functools.partial(backward_kernel, block=block, tq=tq, tk=tk),
        out_shape=jax.ShapeDtypeStruct(qkv.shape, jnp.bfloat16),
        grid_spec=pltpu.PrefetchScalarGridSpec(
            num_scalar_prefetch=1,
            grid=(heads,),
            in_specs=[
                part(0), part(1), part(2), one, one,
                pl.BlockSpec((1, 1, seq), lambda h, _: (h, 0, 0)),
            ]
            + [pl.BlockSpec(memory_space=pl.ANY)] * len(others),
            out_specs=pl.BlockSpec((3 * HEAD_DIM, seq), lambda h, _: (h, 0)),
            scratch_shapes=[pltpu.VMEM((seq, HEAD_DIM), jnp.bfloat16)] * 4
            + [pltpu.VMEM((seq, HEAD_DIM), jnp.float32)] * 2,
        ),
        compiler_params=pltpu.CompilerParams(vmem_limit_bytes=48 * 2**20),
        cost_estimate=pl.CostEstimate(
            flops=heads * seq * seq * 1900, bytes_accessed=heads * seq * 64 * 18,
            transcendentals=heads * seq * seq // 2,
        ),
        name="attn_backward",
    )(here, qkv, qkv, qkv, grad, wide, lse, *others)


eps = 1e-05


def layer_norm(rows, gain, shift):
    average = jnp.mean(rows, axis=-1, keepdims=True)
    centred = rows - average
    variance = jnp.mean(centred * centred, axis=-1, keepdims=True)
    return centred * lax.rsqrt(variance + eps) * gain + shift


def gelu_tanh(values):
    return jax.nn.gelu(values, approximate=True)


def swap(value, axis, step):
    count = lax.axis_size(axis)
    return lax.ppermute(value, axis, [(i, i ^ step) for i in range(count)])


def gather_xor(value, axis):
    count = lax.axis_size(axis)
    held = {0: value}
    step = count // 2
    while step:
        held.update({r ^ step: swap(held[r], axis, step) for r in list(held)})
        step //= 2
    return [held[r] for r in range(count)]


def after(value, *others):
    return lax.optimization_barrier((value,) + others)[0]


def once(value, other):
    return value + (other.reshape(-1)[0] * 0).astype(value.dtype)


def gather_row(value, axis):
    index = lax.axis_index("row")
    parts = gather_xor(value, "row")
    if len(parts) == 2:
        low_part = jnp.where(index == 0, parts[0], parts[1])
        high_part = jnp.where(index == 0, parts[1], parts[0])
        return jnp.concatenate([low_part, high_part], axis)
    stacked = jnp.zeros((len(parts),) + value.shape, value.dtype)
    for step, part in enumerate(parts):
        stacked = lax.dynamic_update_index_in_dim(stacked, part, index ^ step, 0)
    shape = list(value.shape)
    shape[axis] *= len(parts)
    return jnp.moveaxis(stacked, 0, axis).reshape(shape)


def send_blocks(stacked, axis):
    index = lax.axis_index(axis)
    own = lax.dynamic_index_in_dim(stacked, index, 0, keepdims=False)
    parts = []
    for step in range(1, stacked.shape[0]):
        part = lax.dynamic_index_in_dim(stacked, index ^ step, 0, keepdims=False)
        parts.append(swap(part.astype(jnp.bfloat16), axis, step))
    return own, parts


def add_up(own, parts):
    total = own.astype(jnp.float32)
    for part in parts:
        total = total + part.astype(jnp.float32)
    return total


def send_total(total, axis):
    total = total.astype(jnp.bfloat16)
    return [total] + [swap(total, axis, s) for s in range(1, lax.axis_size(axis))]


def place(parts, axis):
    index = lax.axis_index(axis)
    out = jnp.zeros((len(parts),) + parts[0].shape, jnp.float32)
    for step, part in enumerate(parts):
        out = lax.dynamic_update_index_in_dim(out, part.astype(jnp.float32), index ^ step, 0)
    return lax.optimization_barrier(out)


def sum_small(value, axes):
    for axis in axes:
        step = 1
        while step < lax.axis_size(axis):
            value = value + swap(value, axis, step)
            step *= 2
    return value


def contract(left, right, left_dim, right_dim):
    return lax.dot_general(
        left, right, (((left_dim,), (right_dim,)), ((), ())), preferred_element_type=jnp.float32
    )


def body(
    inputs,
    pre_attn_gain,
    pre_attn_shift,
    qkv_weight,
    qv_bias,
    out_weight,
    out_bias,
    pre_mlp_gain,
    pre_mlp_shift,
    fc_weight,
    fc_bias,
    proj_weight,
    proj_bias,
    cotangent,
):
    low = jnp.bfloat16
    wide = jnp.float32
    rows, width = inputs.shape
    cols = lax.axis_size("col")
    row_count = lax.axis_size("row")
    row_index = lax.axis_index("row")
    here = lax.axis_index("col").astype(jnp.int32).reshape(1)
    head_cols = qkv_weight.shape[2]
    hidden_cols = fc_weight.shape[1]
    gain_one, shift_one = pre_attn_gain.astype(wide), pre_attn_shift.astype(wide)
    gain_two, shift_two = pre_mlp_gain.astype(wide), pre_mlp_shift.astype(wide)

    heads = head_cols // HEAD_DIM
    dp_count = lax.axis_size("dp")
    stream = inputs.astype(wide)
    normed_one = layer_norm(stream, gain_one, shift_one).astype(low)
    normed = gather_xor(normed_one, "col")
    qkv_own = qkv_weight.reshape(-1, 3, heads, HEAD_DIM).transpose(2, 1, 3, 0)
    qkv_own = qkv_own.reshape(3 * head_cols, -1)
    qkv_full = gather_row(qkv_own, 1)
    bias_wide = qv_bias.astype(wide)
    bias_rows = jnp.stack([bias_wide[0], jnp.zeros_like(bias_wide[0]), bias_wide[1]])
    bias_col = jnp.swapaxes(bias_rows.reshape(3, heads, HEAD_DIM), 0, 1).reshape(-1, 1)
    normed_near = jnp.concatenate(normed[:2], 0)
    normed_far = jnp.concatenate(normed[2:], 0)
    qkv = jnp.concatenate(
        [
            (contract(qkv_full, part, 1, 1) + bias_col).astype(low)
            for part in (normed_near, normed_far)
        ],
        1,
    )
    if row_count == 2:
        inner = proj_weight.shape[0] // 2
        both = swap(
            jnp.concatenate(
                [fc_weight, jnp.concatenate([proj_weight[:inner], proj_weight[inner:]], 1)], 0
            ),
            "row",
            1,
        )
        fc_pair = (fc_weight, both[: fc_weight.shape[0]])
        proj_there = both[fc_weight.shape[0] :]
        proj_there = jnp.concatenate(
            [proj_there[:, : width // 2], proj_there[:, width // 2 :]], 0
        )
        proj_pair = (proj_weight, proj_there)
        fc_full, proj_full = (
            jnp.concatenate(
                [
                    jnp.where(row_index == 0, pair[0], pair[1]),
                    jnp.where(row_index == 0, pair[1], pair[0]),
                ],
                axis,
            )
            for pair, axis in ((fc_pair, 0), (proj_pair, 1))
        )
    else:
        both = fc_full = gather_row(fc_weight, 0)
        proj_full = gather_row(proj_weight, 1)
    cot_far = swap(once(cotangent, normed[2][0, :1]), "col", 2)
    waits = {1: (both,), 2: (cot_far,)}
    attended = [
        attend_forward(here, qkv, rows, head, 1, waits.get(head, ())) for head in range(heads)
    ]
    context_wide = jnp.concatenate([done[1] for done in attended], 0)
    lse = jnp.concatenate([done[2] for done in attended], 0)
    out_near = gather_row(out_weight, 1)
    out_far = gather_row(swap(once(out_weight, attended[0][2][0, 0, :1]), "col", 2), 1)
    out_full = jnp.concatenate(
        [out_near, swap(out_near, "col", 1), out_far, swap(out_far, "col", 1)], 0
    )
    contexts = [
        jnp.concatenate([done[0][:, r * rows : (r + 1) * rows] for done in attended], 0)
        for r in range(cols)
    ]
    contexts = contexts[:1] + [swap(contexts[r], "col", r) for r in range(1, cols)]
    context_own = jnp.concatenate(contexts, 0)
    mid_stream = stream + contract(context_own, out_full, 0, 0) + out_bias.astype(wide)
    normed_two = layer_norm(mid_stream, gain_two, shift_two).astype(low)
    two_far = swap(normed_two, "col", 2)
    fc_bias_wide = fc_bias.astype(wide)

    def forward_and_back(normed_side, cot_side):
        pre_act = contract(normed_side, fc_full, 1, 0) + fc_bias_wide
        hidden_wide, gelu_pull = jax.vjp(gelu_tanh, pre_act)
        hidden = hidden_wide.astype(low)
        return hidden, gelu_pull(contract(cot_side, proj_full, 1, 1))[0].astype(low)

    def weight_parts(hidden, pre_grad, normed_side, cot_side):
        return (
            contract(normed_side, pre_grad, 0, 0),
            contract(cot_side, hidden, 0, 0),
            jnp.sum(pre_grad, axis=0, dtype=wide),
        )

    near_in = jnp.concatenate([normed_two, swap(normed_two, "col", 1)], 0)
    near_cot = jnp.concatenate([cotangent, swap(cotangent, "col", 1)], 0)
    near_hidden, near_grad = forward_and_back(near_in, near_cot)
    near_one = contract(near_grad[rows:], fc_full, 1, 1).astype(low)
    two_here = contract(near_grad[:rows], fc_full, 1, 1) + swap(near_one, "col", 1).astype(wide)
    mlp_one = contract(near_hidden[rows:], proj_full, 1, 0).astype(low)
    mlp_here = contract(near_hidden[:rows], proj_full, 1, 0) + swap(mlp_one, "col", 1).astype(wide)
    two_far = once(two_far, near_one[0, :1])
    far_in = jnp.concatenate([two_far, swap(two_far, "col", 1)], 0)
    far_cot = jnp.concatenate([cot_far, swap(cot_far, "col", 1)], 0)
    far_hidden, far_grad = forward_and_back(far_in, far_cot)
    far_three = contract(far_grad[rows:], fc_full, 1, 1).astype(low)
    far_two = contract(far_grad[:rows], fc_full, 1, 1) + swap(far_three, "col", 1).astype(wide)
    two_there = far_two.astype(low)
    two_back = swap(two_there, "col", 2)
    near_parts = weight_parts(
        once(near_hidden, two_there[0, :1]), once(near_grad, two_there[0, :1]), near_in, near_cot
    )
    far_parts = weight_parts(far_hidden, far_grad, far_in, far_cot)
    fc_own, fc_parts = send_blocks(
        (near_parts[0] + far_parts[0]).reshape(row_count, -1, hidden_cols), "row"
    )
    proj_own, proj_parts = send_blocks(
        (near_parts[1] + far_parts[1]).reshape(row_count, -1, hidden_cols), "row"
    )
    mlp_three = contract(far_hidden[rows:], proj_full, 1, 0).astype(low)
    mlp_two = contract(far_hidden[:rows], proj_full, 1, 0) + swap(mlp_three, "col", 1).astype(wide)
    mlp_there = mlp_two.astype(low)
    qkv_far = swap(once(qkv_full, two_back[0, :1]), "col", 2)
    qkv_beside = swap(qkv_full, "col", 1)

    normed_two_grad = two_here + two_back.astype(wide)
    out_grad = cotangent.astype(wide)
    norm_two_pull = jax.vjp(layer_norm, mid_stream, gain_two, shift_two)[1]
    stream_two, gain_two_grad, shift_two_grad = norm_two_pull(normed_two_grad)
    mid_grad = out_grad + stream_two
    mid_low = mid_grad.astype(low)
    context_grad_own = contract(out_full, mid_low, 1, 1).astype(low)
    pieces = [context_grad_own[r * head_cols : (r + 1) * head_cols] for r in range(cols)]
    pieces = pieces[:1] + [swap(pieces[r], "col", r) for r in range(1, cols)]
    context_grad = jnp.concatenate(pieces, 1)

    late_low = after(mid_low, context_grad_own)
    out_there = contract(jnp.concatenate([contexts[1], contexts[3]], 0), late_low, 1, 0).astype(low)
    out_recv = swap(out_there, "col", 1)
    fc_own, proj_own = (once(own, context_grad_own[0, :1]) for own in (fc_own, proj_own))
    mlp_block = jnp.stack(
        [
            add_up(fc_own, fc_parts).reshape(dp_count, -1, hidden_cols),
            add_up(proj_own, proj_parts).reshape(dp_count, -1, hidden_cols),
        ],
        1,
    )
    mlp_own, mlp_slices = send_blocks(mlp_block, "dp")
    small_two = jnp.stack(
        [
            jnp.sum(late_low, axis=0, dtype=wide),
            gain_two_grad,
            shift_two_grad,
            jnp.sum(after(out_grad, context_grad_own), axis=0),
        ]
    )
    out_two = contract(contexts[2], late_low, 1, 0) + out_recv[head_cols:].astype(wide)
    out_back = swap(out_two.astype(low), "col", 2)

    grouped = attend_backward(
        here, qkv, context_grad, context_wide, lse, rows, (out_recv, qkv_beside)
    )
    arrived = [grouped[:, r * rows : (r + 1) * rows] for r in range(cols)]
    arrived = arrived[:1] + [swap(arrived[r], "col", r) for r in range(1, cols)]
    mlp_total = add_up(once(mlp_own, grouped[0, :1]), mlp_slices).astype(low)
    mlp_totals = send_total(once(mlp_total, arrived[2][0, :1]), "dp")
    attn_part = jnp.concatenate(
        [
            contract(grouped[:, : 2 * rows], normed_near, 1, 0)
            + contract(grouped[:, 2 * rows :], normed_far, 1, 0),
            contract(contexts[0], late_low, 1, 0)
            + out_recv[:head_cols].astype(wide)
            + out_back.astype(wide),
        ],
        0,
    )
    if row_count == 2:
        half = width // 2
        attn_own = jnp.where(row_index == 0, attn_part[:, :half], attn_part[:, half:])
        sent = jnp.where(row_index == 0, attn_part[:, half:], attn_part[:, :half])
        sent = once(once(sent, mlp_total[0, 0, :1]), qkv_far[0, :1])
        attn_parts = [swap(sent.astype(low), "row", 1)]
    else:
        attn_blocks = jnp.moveaxis(attn_part.reshape(attn_part.shape[0], row_count, -1), 1, 0)
        attn_own, attn_parts = send_blocks(attn_blocks, "row")
    qkv_all = [qkv_full, qkv_beside, qkv_far, swap(qkv_far, "col", 1)]
    normed_one_grad = contract(
        jnp.concatenate(arrived, 0), jnp.concatenate(qkv_all, 0), 0, 0
    )
    attn_block = add_up(attn_own, attn_parts).reshape(dp_count, -1, attn_own.shape[1])
    attn_own, attn_slices = send_blocks(attn_block, "dp")
    norm_one_pull = jax.vjp(layer_norm, stream, gain_one, shift_one)[1]
    stream_one, gain_one_grad, shift_one_grad = norm_one_pull(normed_one_grad)
    input_grad = (mid_grad + stream_one).astype(low)
    small = jnp.concatenate([jnp.stack([gain_one_grad, shift_one_grad]), small_two], 0)
    small = sum_small(small, ("col",))
    qv_part = jnp.sum(grouped.astype(wide), axis=1).reshape(heads, 3, HEAD_DIM)
    qv_part = jnp.swapaxes(qv_part, 0, 1)[0::2].reshape(-1)
    extra = jnp.concatenate([qv_part, near_parts[2] + far_parts[2]])
    extra = jnp.pad(extra, (0, -extra.shape[0] % width)).reshape(-1, width)
    small = sum_small(jnp.concatenate([small, extra], 0), ("row", "dp"))
    extra = small[6:].reshape(-1)
    attn_sum = place(send_total(add_up(attn_own, attn_slices), "dp"), "dp")
    attn_sum = attn_sum.reshape(-1, attn_own.shape[1])
    qkv_sum = attn_sum[: 3 * head_cols].reshape(heads, 3, HEAD_DIM, -1)
    mlp_sums = place(mlp_totals, "dp")
    mlp_back = swap(after(mlp_there, arrived[2]), "col", 2)
    block_out = mid_stream + mlp_here + mlp_back.astype(wide) + proj_bias.astype(wide)
    return (
        block_out.astype(low),
        input_grad,
        small[0],
        small[1],
        qkv_sum.transpose(3, 1, 0, 2).reshape(qkv_weight.shape),
        extra[: 2 * head_cols].reshape(2, head_cols),
        attn_sum[3 * head_cols :],
        small[2],
        small[3],
        small[4],
        mlp_sums[:, 0].reshape(fc_weight.shape),
        extra[2 * head_cols : 2 * head_cols + hidden_cols],
        mlp_sums[:, 1].reshape(-1, hidden_cols).T,
        small[5],
    )


def solution(mesh):
    placed = (
        P(("dp", "row", "col"), None),
        P(),
        P(),
        P("row", None, "col"),
        P(None, "col"),
        P("col", "row"),
        P(),
        P(),
        P(),
        P("row", "col"),
        P("col"),
        P("col", "row"),
        P(),
        P(("dp", "row", "col"), None),
    )
    return jax.shard_map(
        body,
        mesh=mesh,
        in_specs=placed,
        out_specs=(
            P(("dp", "row", "col"), None),
            P(("dp", "row", "col"), None),
            P(),
            P(),
            P("row", None, "col"),
            P(None, "col"),
            P("col", "row"),
            P(),
            P(),
            P(),
            P("row", "col"),
            P("col"),
            P("col", "row"),
            P(),
        ),
        check_vma=False,
    )
```
